256 devices in a mesh: row: 8 (over y, x_lo), col: 32 (over z, x_hi, core).
Axes of the slice: x: 4 (x_hi: 2, x_lo: 2; x = x_hi * 2 + x_lo), y: 4, z: 8, core: 2. Of those that a mesh axis runs over, the one named last changes fastest.
Arguments:
- q_load: bfloat16 [8, 4096, 4096], P('row', 'col'), may hold values from -160 to 160
- k_load: bfloat16 [8, 4096, 512], P('row', 'col'), may hold values from -160 to 160
- v_load: bfloat16 [8, 4096, 512], P('row', 'col'), may hold values from -6 to 6
- q_bias: float32 [4096], replicated, may hold values from -3 to 3
- k_bias: float32 [512], replicated, may hold values from -3 to 3
- v_bias: float32 [512], replicated, may hold values from -3 to 3
- place: int32 [8, 4096], P('row', 'col'), may hold values from 0 to 4095, as said below
- segment: int32 [8, 4096], P('row', 'col'), may hold values from 0 to 7, never falling along the last dimension, each value on 1 to 1024 neighbouring positions
- d_context: bfloat16 [8, 4096, 4096], P('row', 'col'), may hold values from -6 to 6
Outputs:
- context: bfloat16 [8, 4096, 4096], P('row', 'col')
- grad_q: bfloat16 [8, 4096, 4096], P('row', 'col')
- grad_k: bfloat16 [8, 4096, 512], P('row', 'col')
- grad_v: bfloat16 [8, 4096, 512], P('row', 'col')
- bias_grad_q: float32 [4096], P(('row', 'col'))
- bias_grad_kv: float32 [2, 512], P(None, ('row', 'col'))
The draws below stay inside these ranges and needn't reach their ends.
Inputs may be any that keep to these rules, and one draw needn't show every extreme that they name: `place`: in each group every position appears once, and each device holds the same number of rows for each device of its col group. `segment`: in each group the numbers never fall, every sample covers 1 to 1024 positions and one covers exactly 1024; every number appears.
All inputs are finite; a program needn't handle non-finite values.
Results may differ from the reference program's by a relative error of at most 0.034.
Values may be sent and summed in bfloat16 or wider, within the bound.
No kernel may reach another device: no remote copies, remote signals or barrier semaphores. Data moves between devices by JAX's collectives and lax.ppermute only.
A program may use at most 64 MiB of HBM per device.

```python
import math
import jax
import jax.numpy as jnp
import numpy as np
from jax import lax

HEADS = 32
KV_HEADS = 4
HEAD_DIM = 128
TOK_DEV = 128
BLOCK = 512
SEQ = 4096
MOST_LEN = 1024
SEGS = 8
N_ROW = 8
N_COL = 32


def place_table(key):
    base = jax.random.fold_in(key, 11)
    bucket = TOK_DEV // N_COL
    first_key, second_key = jax.random.split(base)
    keys_one = jax.random.split(first_key, N_ROW * N_COL)
    slots = jax.vmap(lambda subkey: jax.random.permutation(subkey, TOK_DEV))(keys_one)
    slots = slots.reshape(N_ROW, N_COL, N_COL, bucket).astype(jnp.int32)
    shifts = (jnp.arange(N_COL, dtype=jnp.int32) * TOK_DEV).reshape(1, N_COL, 1, 1)
    slots = jnp.transpose(slots + shifts, (0, 2, 1, 3)).reshape(N_ROW, N_COL, TOK_DEV)
    keys_two = jax.random.split(second_key, N_ROW * N_COL)
    mixing = jax.vmap(lambda subkey: jax.random.permutation(subkey, TOK_DEV))(keys_two)
    mixing = mixing.reshape(N_ROW, N_COL, TOK_DEV).astype(jnp.int32)
    slots = jnp.take_along_axis(slots, mixing, axis=2)
    return slots.reshape(N_ROW, SEQ)


def draw_place(key, part):
    return place_table(key)


def draw_q_load(key, part):
    key = jax.random.fold_in(key, 31)
    return jnp.clip(jax.random.normal(key, (N_ROW, SEQ, HEADS * HEAD_DIM), jnp.float32), -6.0, 6.0).astype(jnp.bfloat16)


def draw_k_load(key, part):
    key = jax.random.fold_in(key, 37)
    return jnp.clip(jax.random.normal(key, (N_ROW, SEQ, KV_HEADS * HEAD_DIM), jnp.float32), -6.0, 6.0).astype(jnp.bfloat16)


def block_levels(key, extent, cuts, low, high):
    gain = 1.0
    for axis_at, parts in cuts:
        heights = jax.random.uniform(jax.random.fold_in(jax.random.fold_in(key, 6), axis_at), (parts,), jnp.float32, low / len(cuts), high / len(cuts))
        gain = gain * jnp.repeat(jnp.exp(heights), extent[axis_at] // parts).reshape((-1,) + (1,) * (len(extent) - 1 - axis_at))
    return gain


def length_profile(amount, total, bound, slope):
    portions = [(1 << 20) // math.isqrt(standing ** slope) + 1 for standing in range(2, amount + 1)]
    surplus, holding = total - bound - (amount - 1), [1] * (amount - 1)
    while surplus > 0:
        free = [i for i in range(amount - 1) if holding[i] < bound]
        whole, left = sum([portions[i] for i in free]), surplus
        for i in free:
            more = min(bound - holding[i], max(1, left * portions[i] // whole), surplus)
            holding[i] = holding[i] + more
            surplus = surplus - more
    return np.array([bound] + holding)


def ragged(key, number_of, total, limit, slope):
    if number_of == 2:
        one = jax.random.randint(key, (), max(1, total - limit), min(limit, total - 1) + 1)
        return jnp.stack([one, total - one])
    lengths = jnp.asarray(length_profile(number_of, total, limit, slope), jnp.int32)
    twos = (number_of - 1) // 2
    donor, receiver = lengths[1:1 + 2 * twos:2], lengths[2:2 + 2 * twos:2]
    margin = jnp.minimum(donor - 1, limit - receiver)
    shifted = jax.random.randint(jax.random.fold_in(key, 1), (twos,), 0, 1 << 20) % (margin + 1)
    lengths = lengths.at[1:1 + 2 * twos:2].set(donor - shifted).at[2:2 + 2 * twos:2].set(receiver + shifted)
    return lengths[jax.random.permutation(jax.random.fold_in(key, 2), number_of)]


def bell_draw(stream_key, shape, spread, bound, shards=(), kind=jnp.bfloat16):
    gain = block_levels(stream_key, shape, shards, -0.22, 0.18) if shards else 1.0
    drawn = jax.random.normal(stream_key, shape, jnp.float32) * spread * gain
    return jnp.minimum(jnp.maximum(drawn, -bound), bound).astype(kind)


def setup_inputs(seed: int = 0) -> dict:
    key_list = jax.random.split(jax.random.key(seed), 10)
    q_load = draw_q_load(jax.random.fold_in(key_list[9], 71), 0)
    k_load = draw_k_load(jax.random.fold_in(key_list[9], 71), 0)
    v_load = bell_draw(key_list[2], (N_ROW, SEQ, KV_HEADS * HEAD_DIM), 1.0, 6.0, ((0, 8), (1, 32)))
    q_bias = bell_draw(key_list[3], (HEADS * HEAD_DIM,), 0.5, 3.0, (), jnp.float32)
    k_bias = bell_draw(key_list[4], (KV_HEADS * HEAD_DIM,), 0.5, 3.0, (), jnp.float32)
    v_bias = bell_draw(key_list[5], (KV_HEADS * HEAD_DIM,), 0.5, 3.0, (), jnp.float32)
    place = draw_place(jax.random.fold_in(key_list[9], 71), 0)
    segment = jax.vmap(lambda own: jnp.searchsorted(jnp.cumsum(ragged(own, SEGS, SEQ, MOST_LEN, 2)), jnp.arange(SEQ), side="right"))(jax.random.split(key_list[7], N_ROW)).reshape((N_ROW, SEQ)).astype(jnp.int32)
    d_context = bell_draw(key_list[8], (N_ROW, SEQ, HEADS * HEAD_DIM), 1.0, 6.0, ((0, 8), (1, 32)))
    return dict(q_load=q_load, k_load=k_load, v_load=v_load, q_bias=q_bias, k_bias=k_bias, v_bias=v_bias, place=place, segment=segment, d_context=d_context)


ROPE_BASE = 1000000.0
MASKED = -1.0e30


def rotation(segment, width):
    length = segment.shape[0]
    index = jnp.arange(length, dtype=jnp.int32)
    change = jnp.concatenate([jnp.ones((1,), dtype=jnp.bool_), segment[1:] != segment[:-1]])
    begins = lax.cummax(jnp.where(change, index, jnp.zeros_like(index)), axis=0)
    offset = (index - begins).astype(jnp.float32)
    powers = jnp.arange(width // 2, dtype=jnp.float32) * (2.0 / width)
    rates = ROPE_BASE ** (-powers)
    angle = offset[:, None] * rates[None, :]
    return jnp.cos(angle), jnp.sin(angle)


def rotate(values, cosine, sine, sign):
    half = values.shape[-1] // 2
    front = values[..., :half]
    back = values[..., half:]
    turn_cos = cosine[:, None, :]
    turn_sin = sign * sine[:, None, :]
    return jnp.concatenate([front * turn_cos - back * turn_sin, back * turn_cos + front * turn_sin], axis=-1)


def head_pass(query, keys, values, upstream, segment, scale):
    length, width = query.shape
    window = BLOCK + MOST_LEN
    pad_keys = jnp.concatenate([jnp.zeros((MOST_LEN, width), keys.dtype), keys])
    pad_values = jnp.concatenate([jnp.zeros((MOST_LEN, width), values.dtype), values])
    pad_segment = jnp.concatenate([jnp.full((MOST_LEN,), -1, jnp.int32), segment.astype(jnp.int32)])

    def visit(carry, block):
        grad_keys, grad_values = carry
        start = block * BLOCK
        q_part = lax.dynamic_slice_in_dim(query, start, BLOCK, 0)
        up_part = lax.dynamic_slice_in_dim(upstream, start, BLOCK, 0)
        seg_rows = lax.dynamic_slice_in_dim(segment.astype(jnp.int32), start, BLOCK, 0)
        k_part = lax.dynamic_slice_in_dim(pad_keys, start, window, 0)
        v_part = lax.dynamic_slice_in_dim(pad_values, start, window, 0)
        seg_cols = lax.dynamic_slice_in_dim(pad_segment, start, window, 0)
        row_pos = start + jnp.arange(BLOCK, dtype=jnp.int32)
        col_pos = start - MOST_LEN + jnp.arange(window, dtype=jnp.int32)
        allowed = (seg_rows[:, None] == seg_cols[None, :]) & (col_pos[None, :] <= row_pos[:, None])
        scores = lax.dot_general(q_part, k_part, (((1,), (1,)), ((), ())), preferred_element_type=jnp.float32) * scale
        scores = jnp.where(allowed, scores, MASKED)
        top = jnp.max(scores, axis=1, keepdims=True)
        weights = jnp.where(allowed, jnp.exp(scores - top), 0.0)
        prob = weights / jnp.sum(weights, axis=1, keepdims=True)
        prob_low = prob.astype(jnp.bfloat16)
        output = jnp.dot(prob_low, v_part, preferred_element_type=jnp.float32).astype(jnp.bfloat16)
        delta = jnp.sum(up_part.astype(jnp.float32) * output.astype(jnp.float32), axis=1, keepdims=True)
        grad_prob = lax.dot_general(up_part, v_part, (((1,), (1,)), ((), ())), preferred_element_type=jnp.float32)
        grad_score = (prob * (grad_prob - delta)).astype(jnp.bfloat16)
        grad_query = jnp.dot(grad_score, k_part, preferred_element_type=jnp.float32) * scale
        key_term = lax.dot_general(grad_score, q_part, (((0,), (0,)), ((), ())), preferred_element_type=jnp.float32) * scale
        value_term = lax.dot_general(prob_low, up_part, (((0,), (0,)), ((), ())), preferred_element_type=jnp.float32)
        grad_keys = lax.dynamic_update_slice_in_dim(grad_keys, lax.dynamic_slice_in_dim(grad_keys, start, window, 0) + key_term, start, 0)
        grad_values = lax.dynamic_update_slice_in_dim(grad_values, lax.dynamic_slice_in_dim(grad_values, start, window, 0) + value_term, start, 0)
        return (grad_keys, grad_values), (output, grad_query)

    init = (jnp.zeros((length + MOST_LEN, width), jnp.float32), jnp.zeros((length + MOST_LEN, width), jnp.float32))
    carry, stacked = lax.scan(visit, init, jnp.arange(length // BLOCK, dtype=jnp.int32))
    outputs = stacked[0].reshape(length, width)
    grad_queries = stacked[1].reshape(length, width)
    return outputs, grad_queries, carry[0][MOST_LEN:], carry[1][MOST_LEN:]


def reference(q_load, k_load, v_load, q_bias, k_bias, v_bias, place, segment, d_context):
    group_size = HEADS // KV_HEADS
    scale = HEAD_DIM ** -0.5
    kv_width = KV_HEADS * HEAD_DIM
    q_gain = q_bias.reshape(HEADS, HEAD_DIM)
    k_gain = k_bias.reshape(KV_HEADS, HEAD_DIM)
    v_gain = v_bias.reshape(KV_HEADS, HEAD_DIM)

    def one_group(items):
        q_rows, k_rows, v_rows, slots, sample_ids, upstream = items
        arrange = jnp.argsort(slots)
        cosine, sine = rotation(sample_ids, HEAD_DIM)
        q_plan = q_rows[arrange].reshape(SEQ, HEADS, HEAD_DIM).astype(jnp.float32) + q_gain
        q_rot = rotate(q_plan, cosine, sine, 1.0).astype(jnp.bfloat16)
        k_plan = k_rows[arrange].reshape(SEQ, KV_HEADS, HEAD_DIM).astype(jnp.float32) + k_gain
        k_rot = rotate(k_plan, cosine, sine, 1.0).astype(jnp.bfloat16)
        v_val = (v_rows[arrange].reshape(SEQ, KV_HEADS, HEAD_DIM).astype(jnp.float32) + v_gain).astype(jnp.bfloat16)
        up_rows = upstream.reshape(SEQ, HEADS, HEAD_DIM)

        def one_head(head):
            shared = head // group_size
            return head_pass(q_rot[:, head], k_rot[:, shared], v_val[:, shared], up_rows[:, head], sample_ids, scale)

        outputs, grad_queries, grad_keys, grad_values = lax.map(one_head, jnp.arange(HEADS, dtype=jnp.int32))
        context = jnp.transpose(outputs, (1, 0, 2)).reshape(SEQ, HEADS * HEAD_DIM)
        dq_pre = rotate(jnp.transpose(grad_queries, (1, 0, 2)), cosine, sine, -1.0)
        dk_pre = rotate(jnp.transpose(grad_keys, (1, 0, 2)), cosine, sine, -1.0)
        dv_part = jnp.transpose(grad_values, (1, 0, 2))
        k_low = lax.optimization_barrier(dk_pre.astype(jnp.bfloat16)).astype(jnp.float32)
        v_low = lax.optimization_barrier(dv_part.astype(jnp.bfloat16)).astype(jnp.float32)
        k_total = k_low.reshape(SEQ, KV_HEADS, group_size, HEAD_DIM).sum(axis=2).astype(jnp.bfloat16).reshape(SEQ, kv_width)
        v_total = v_low.reshape(SEQ, KV_HEADS, group_size, HEAD_DIM).sum(axis=2).astype(jnp.bfloat16).reshape(SEQ, kv_width)
        grad_q = dq_pre.astype(jnp.bfloat16).reshape(SEQ, HEADS * HEAD_DIM)[slots]
        grad_k = k_total[slots]
        grad_v = v_total[slots]
        bias_q = jnp.sum(dq_pre, axis=0).reshape(HEADS * HEAD_DIM)
        bias_k = jnp.sum(dk_pre, axis=0).reshape(KV_HEADS, group_size, HEAD_DIM).sum(axis=1).reshape(kv_width)
        bias_v = jnp.sum(dv_part, axis=0).reshape(KV_HEADS, group_size, HEAD_DIM).sum(axis=1).reshape(kv_width)
        return context, grad_q, grad_k, grad_v, bias_q, jnp.stack([bias_k, bias_v])

    results = lax.map(one_group, (q_load, k_load, v_load, place, segment, d_context))
    return (results[0], results[1], results[2], results[3], jnp.sum(results[4], axis=0), jnp.sum(results[5], axis=0))
```

```python
import functools

import jax
import jax.numpy as jnp
from jax import lax
from jax.experimental import pallas as pl
from jax.experimental.pallas import tpu as pltpu
from jax.sharding import PartitionSpec as P

HEADS = 32
KV_HEADS = 4
GROUP = 8
HEAD_DIM = 128
SEGS = 8
TOK = 128
SLAB = 512
QBLK = 256
KTILE = 256
WINDOW = 1280
Q_WIDTH = HEADS * HEAD_DIM
KV_WIDTH = KV_HEADS * HEAD_DIM
PART = GROUP * HEAD_DIM
SENT = PART + 6 * HEAD_DIM + 128
BACK = PART + 6 * HEAD_DIM
MIB = 1024 * 1024

ROPE_BASE = 1000000.0
MASKED = -1e30
LOG2E = 1.4426950408889634
F32 = jnp.float32
BF16 = jnp.bfloat16

NN = (((1,), (0,)), ((), ()))
NT = (((1,), (1,)), ((), ()))


def dot(a, b, dims=NN):
    return lax.dot_general(a, b, dims, preferred_element_type=F32)


def iota(shape, axis):
    return lax.broadcasted_iota(jnp.int32, shape, axis)


def row_to_column(row, size):
    same = iota((size, size), 0) == iota((size, size), 1)
    return jnp.sum(jnp.where(same, row, 0.0), axis=1, keepdims=True)


def pack_kernel(q_ref, k_ref, v_ref, place_ref, seg_ref, out_ref):
    place_row = place_ref[...].astype(F32)
    place_col = row_to_column(place_row, TOK)
    rank = jnp.sum(jnp.where(place_col < place_row, 1.0, 0.0), axis=0, keepdims=True)
    pick = iota((TOK, TOK), 0).astype(F32) == rank
    pick_low = jnp.where(pick, 1.0, 0.0).astype(BF16)
    ranked = jnp.sum(jnp.where(pick, place_row, 0.0), axis=1, keepdims=True)
    inside = ranked - ((iota((TOK, 1), 0) // 16) * SLAB).astype(F32)
    high = jnp.floor(inside * (1.0 / 128.0))
    low = inside - 128.0 * high
    seg_col = row_to_column(seg_ref[...].astype(F32), TOK)
    lane = iota((TOK, 128), 1)
    below = jnp.sum(
        jnp.where(seg_col < (lane - 8).astype(F32), 1.0, 0.0), axis=0, keepdims=True
    )
    lane16 = iota((16, 128), 1)
    counts = jnp.where(iota((16, 128), 0) == 0, below, 0.0)
    for j in range(KV_HEADS):
        part = dot(pick_low, q_ref[:, PART * j : PART * (j + 1)]).astype(BF16)
        for z in range(8):
            out_ref[4 * z + j, :, 0:PART] = part[16 * z : 16 * z + 16]
    keys = dot(pick_low, k_ref[...]).astype(BF16)
    vals = dot(pick_low, v_ref[...]).astype(BF16)
    for z in range(8):
        meta = counts
        for t in range(3):
            s = (z - 2 + t) % 8
            rows = slice(16 * s, 16 * s + 16)
            meta = jnp.where(lane16 == 2 * t, high[rows], meta)
            meta = jnp.where(lane16 == 2 * t + 1, low[rows], meta)
            base = PART + 256 * t
            for j in range(KV_HEADS):
                head = slice(HEAD_DIM * j, HEAD_DIM * (j + 1))
                out_ref[4 * z + j, :, base : base + 128] = keys[rows, head]
                out_ref[4 * z + j, :, base + 128 : base + 256] = vals[rows, head]
        for j in range(KV_HEADS):
            out_ref[4 * z + j, :, BACK:SENT] = meta.astype(BF16)


def turn(values, cosine, sine):
    return values * cosine + pltpu.roll(values, HEAD_DIM // 2, 1) * sine


def unturn(values, cosine, sine):
    return values * cosine - pltpu.roll(values, HEAD_DIM // 2, 1) * sine


def attend_kernel(
    col_ref, recv_ref, up0, up1, up2, up3, qb_ref, kb_ref, vb_ref, cos_ref, sin_ref,
    ctx0, ctx1, ctx2, ctx3, back_ref, bias_ref,
    up_s, q_s, k_s, v_s, kt_s, vt_s, cos_s, sin_s, mask_s, s_s, p_s, dk_s, dv_s, ctx_s, dq_s,
):
    col = col_ref[0]
    z = col // 4
    j = col % 4
    first = SLAB * (z - 2)
    scale = HEAD_DIM ** (-0.5)

    for s, ref in enumerate((up0, up1, up2, up3)):
        up_s[pl.ds(pl.multiple_of(TOK * (j ^ s), TOK), TOK), :] = ref[...]

    meta = recv_ref[:, BACK:SENT].astype(F32)
    meta_rows = jnp.transpose(meta)
    starts = [jnp.sum(meta[:, 8 + v : 9 + v]).astype(jnp.int32) for v in range(SEGS)]

    for b in range(12):
        at = first + TOK * b
        rows = slice(TOK * b, TOK * (b + 1))
        for v in range(SEGS):
            begin = starts[v]
            end = starts[v + 1] if v + 1 < SEGS else jnp.int32(8 * SLAB)
            if v == 0:
                cos_s[rows, :] = jnp.zeros((TOK, HEAD_DIM), F32)
                sin_s[rows, :] = jnp.zeros((TOK, HEAD_DIM), F32)

            @pl.when((begin < at + TOK) & (end > at))
            def _():
                src = pl.ds(at - begin + TOK, TOK)
                inside = at + iota((TOK, HEAD_DIM), 0) >= begin
                cos_s[rows, :] = jnp.where(inside, cos_ref[src, :], cos_s[rows, :])
                sin_s[rows, :] = jnp.where(inside, sin_ref[src, :], sin_s[rows, :])

    k_bias = kb_ref[:, pl.ds(pl.multiple_of(HEAD_DIM * j, HEAD_DIM), HEAD_DIM)]
    v_bias = vb_ref[:, pl.ds(pl.multiple_of(HEAD_DIM * j, HEAD_DIM), HEAD_DIM)]
    q_bias = qb_ref[:, pl.ds(pl.multiple_of(PART * j, PART), PART)]
    spot = iota((SLAB, SLAB), 0).astype(F32)
    for t in range(3):
        pos = meta_rows[2 * t : 2 * t + 1] * 128.0 + meta_rows[2 * t + 1 : 2 * t + 2]
        pick = jnp.where(spot == pos, 1.0, 0.0).astype(BF16)
        rows = slice(SLAB * t, SLAB * (t + 1))
        base = PART + 256 * t
        both = dot(pick, recv_ref[:, base : base + 256])
        keys = turn(both[:, :128] + k_bias, cos_s[rows, :], sin_s[rows, :])
        vals = both[:, 128:] + v_bias
        k_s[rows, :] = keys.astype(BF16)
        v_s[rows, :] = vals.astype(BF16)
        kt_s[:, rows] = jnp.transpose(keys).astype(BF16)
        vt_s[:, rows] = jnp.transpose(vals).astype(BF16)
        if t == 2:
            for pair in range(4):
                lanes = slice(256 * pair, 256 * (pair + 1))
                both = dot(pick, recv_ref[:, lanes]) + q_bias[:, lanes]
                for u in range(2):
                    one = both[:, 128 * u : 128 * (u + 1)]
                    q_s[2 * pair + u] = turn(one, cos_s[rows, :], sin_s[rows, :]).astype(BF16)

    for i in range(2):
        here = SLAB * z + QBLK * i + iota((1, QBLK), 1)
        begin = jnp.zeros((1, QBLK), jnp.int32)
        for v in range(1, SEGS):
            begin = jnp.where(here >= starts[v], jnp.maximum(begin, starts[v]), begin)
        there = first + QBLK * i + iota((WINDOW, 1), 0)
        mask_s[i] = jnp.where((there >= begin) & (there <= here), 0.0, MASKED)

    dk_s[...] = jnp.zeros_like(dk_s)
    dv_s[...] = jnp.zeros_like(dv_s)
    tiles = WINDOW // KTILE

    def one_head(h, _):
        lanes = pl.ds(pl.multiple_of(h * HEAD_DIM, HEAD_DIM), HEAD_DIM)
        for i in range(2):
            q_rows = slice(QBLK * i, QBLK * (i + 1))
            query = q_s[h, q_rows, :]
            up = up_s[q_rows, lanes]
            up_t = jnp.transpose(up.astype(F32))
            top = None
            for t in range(tiles):
                k_rows = slice(QBLK * i + KTILE * t, QBLK * i + KTILE * (t + 1))
                tile = slice(KTILE * t, KTILE * (t + 1))
                score = dot(k_s[k_rows, :], query, NT) * (scale * LOG2E) + mask_s[i, tile, :]
                s_s[tile, :] = score
                peak = jnp.max(score, axis=0, keepdims=True)
                top = peak if top is None else jnp.maximum(top, peak)
            total = None
            for t in range(tiles):
                tile = slice(KTILE * t, KTILE * (t + 1))
                weight = jnp.exp2(s_s[tile, :] - top)
                s_s[tile, :] = weight
                share = jnp.sum(weight, axis=0, keepdims=True)
                total = share if total is None else total + share
            invert = 1.0 / total
            out_t = None
            for t in range(tiles):
                k_rows = slice(QBLK * i + KTILE * t, QBLK * i + KTILE * (t + 1))
                tile = slice(KTILE * t, KTILE * (t + 1))
                prob = s_s[tile, :] * invert
                s_s[tile, :] = prob
                prob_low = prob.astype(BF16)
                term = dot(vt_s[:, k_rows], prob_low)
                out_t = term if out_t is None else out_t + term
                dv_s[k_rows, :] += dot(prob_low, up)
                p_s[tile, :] = dot(v_s[k_rows, :], up, NT)
            out_low = out_t.astype(BF16).astype(F32)
            ctx_s[q_rows, lanes] = jnp.transpose(out_low).astype(BF16)
            delta = jnp.sum(up_t * out_low, axis=0, keepdims=True)
            dq_t = None
            for t in range(tiles):
                k_rows = slice(QBLK * i + KTILE * t, QBLK * i + KTILE * (t + 1))
                tile = slice(KTILE * t, KTILE * (t + 1))
                dscore = (s_s[tile, :] * (p_s[tile, :] - delta)).astype(BF16)
                term = dot(kt_s[:, k_rows], dscore)
                dq_t = term if dq_t is None else dq_t + term
                dk_s[k_rows, :] += dot(dscore, query)
            dq = jnp.transpose(dq_t) * scale
            w_rows = slice(2 * SLAB + QBLK * i, 2 * SLAB + QBLK * (i + 1))
            dq = unturn(dq, cos_s[w_rows, :], sin_s[w_rows, :])
            dq_s[q_rows, lanes] = dq.astype(BF16)
            mine = jnp.sum(dq, axis=0, keepdims=True)
            if i == 0:
                bias_ref[pl.ds(h, 1), :] = mine
            else:
                bias_ref[pl.ds(h, 1), :] += mine
        return 0

    lax.fori_loop(0, GROUP, one_head, 0)

    for s, ref in enumerate((ctx0, ctx1, ctx2, ctx3)):
        ref[...] = ctx_s[pl.ds(pl.multiple_of(TOK * (j ^ s), TOK), TOK), :]

    sum_k = jnp.zeros((1, HEAD_DIM), F32)
    sum_v = jnp.zeros((1, HEAD_DIM), F32)
    across = iota((SLAB, SLAB), 1).astype(F32)
    for t in range(3):
        rows = slice(SLAB * t, SLAB * (t + 1))
        pos = meta[:, 2 * t : 2 * t + 1] * 128.0 + meta[:, 2 * t + 1 : 2 * t + 2]
        drop = jnp.where(across == pos, 1.0, 0.0).astype(BF16)
        dk = unturn(dk_s[rows, :] * scale, cos_s[rows, :], sin_s[rows, :])
        dv = dv_s[rows, :]
        sum_k = sum_k + jnp.sum(dk, axis=0, keepdims=True)
        sum_v = sum_v + jnp.sum(dv, axis=0, keepdims=True)
        base = PART + 256 * t
        both = jnp.concatenate([dk.astype(BF16), dv.astype(BF16)], axis=1)
        back_ref[:, base : base + 256] = dot(drop, both).astype(BF16)
        if t == 2:
            for pair in range(4):
                lanes = slice(256 * pair, 256 * (pair + 1))
                back_ref[:, lanes] = dot(drop, dq_s[:, lanes]).astype(BF16)
    bias_ref[8:9, :] = sum_k
    bias_ref[9:10, :] = sum_v
    bias_ref[10:16, :] = jnp.zeros((6, HEAD_DIM), F32)


def join_kernel(col_ref, c0, c1, c2, c3, out_ref):
    j = col_ref[0] % 4
    for s, ref in enumerate((c0, c1, c2, c3)):
        out_ref[:, pl.ds(pl.multiple_of(PART * (j ^ s), PART), PART)] = ref[...]


def unpack_kernel(back_ref, place_ref, gq_ref, gk_ref, gv_ref, q_s, k_s, v_s):
    place_row = place_ref[...].astype(F32)
    place_col = row_to_column(place_row, TOK)
    rank = jnp.sum(jnp.where(place_row < place_col, 1.0, 0.0), axis=1, keepdims=True)
    pick = jnp.where(iota((TOK, TOK), 1).astype(F32) == rank, 1.0, 0.0).astype(BF16)
    for j in range(KV_HEADS):
        head = slice(HEAD_DIM * j, HEAD_DIM * (j + 1))
        for s in range(8):
            rows = slice(16 * s, 16 * s + 16)
            q_s[rows, :] = back_ref[4 * s + j, :, 0:PART]
            total = None
            for t in range(3):
                base = PART + 256 * t
                term = back_ref[4 * ((s + 2 - t) % 8) + j, :, base : base + 256].astype(F32)
                total = term if total is None else total + term
            k_s[rows, head] = total[:, :128].astype(BF16)
            v_s[rows, head] = total[:, 128:].astype(BF16)
        gq_ref[:, PART * j : PART * (j + 1)] = dot(pick, q_s[...]).astype(BF16)
    gk_ref[...] = dot(pick, k_s[...]).astype(BF16)
    gv_ref[...] = dot(pick, v_s[...]).astype(BF16)


def vmem_spec():
    return pl.BlockSpec(memory_space=pltpu.VMEM)


def shape(dims, dtype):
    return jax.ShapeDtypeStruct(dims, dtype)


def swap(values, axis, step, size):
    return lax.ppermute(values, axis, [(c, c ^ step) for c in range(size)])


def rotation_tables():
    offset = jnp.arange(-TOK, 1024 + TOK, dtype=jnp.int32).astype(F32)
    powers = jnp.arange(HEAD_DIM // 2, dtype=F32) * (2.0 / HEAD_DIM)
    rates = ROPE_BASE ** (-powers)
    angle = offset[:, None] * rates[None, :]
    cosine = jnp.cos(angle)
    sine = jnp.sin(angle)
    return (
        jnp.concatenate([cosine, cosine], axis=1),
        jnp.concatenate([-sine, sine], axis=1),
    )


def per_device(q_load, k_load, v_load, q_bias, k_bias, v_bias, place, segment, d_context):
    col = lax.axis_index("col")
    row = lax.axis_index("row")
    j = col % 4
    col_arr = col.reshape(1).astype(jnp.int32)
    smem = pl.BlockSpec(memory_space=pltpu.SMEM)

    packed = pl.pallas_call(
        pack_kernel,
        out_shape=shape((32, 16, SENT), BF16),
        in_specs=[vmem_spec()] * 5,
        out_specs=vmem_spec(),
        compiler_params=pltpu.CompilerParams(vmem_limit_bytes=24 * MIB),
        cost_estimate=pl.CostEstimate(flops=2 * 128 * 128 * 5120, bytes_accessed=5 * MIB, transcendentals=0),
    )(q_load[0], k_load[0], v_load[0], place, segment)
    recv = lax.all_to_all(packed, "col", split_axis=0, concat_axis=0, tiled=True)

    up_own = d_context[0]
    ups = []
    for s in range(4):
        piece = lax.dynamic_slice_in_dim(up_own, PART * (j ^ s), PART, 1)
        ups.append(piece if s == 0 else swap(piece, "col", s, 32))
    cos_table, sin_table = rotation_tables()

    attended = pl.pallas_call(
        attend_kernel,
        out_shape=[shape((TOK, PART), BF16)] * 4
        + [shape((SLAB, BACK), BF16), shape((16, HEAD_DIM), F32)],
        in_specs=[smem] + [vmem_spec()] * 10,
        out_specs=[vmem_spec()] * 6,
        scratch_shapes=[
            pltpu.VMEM((SLAB, PART), BF16),
            pltpu.VMEM((GROUP, SLAB, HEAD_DIM), BF16),
            pltpu.VMEM((3 * SLAB, HEAD_DIM), BF16),
            pltpu.VMEM((3 * SLAB, HEAD_DIM), BF16),
            pltpu.VMEM((HEAD_DIM, 3 * SLAB), BF16),
            pltpu.VMEM((HEAD_DIM, 3 * SLAB), BF16),
            pltpu.VMEM((3 * SLAB, HEAD_DIM), F32),
            pltpu.VMEM((3 * SLAB, HEAD_DIM), F32),
            pltpu.VMEM((2, WINDOW, QBLK), F32),
            pltpu.VMEM((WINDOW, QBLK), F32),
            pltpu.VMEM((WINDOW, QBLK), F32),
            pltpu.VMEM((3 * SLAB, HEAD_DIM), F32),
            pltpu.VMEM((3 * SLAB, HEAD_DIM), F32),
            pltpu.VMEM((SLAB, PART), BF16),
            pltpu.VMEM((SLAB, PART), BF16),
        ],
        compiler_params=pltpu.CompilerParams(vmem_limit_bytes=56 * MIB),
        cost_estimate=pl.CostEstimate(flops=8 * 10**9, bytes_accessed=8 * MIB, transcendentals=5 * 10**6),
    )(
        col_arr, recv.reshape(SLAB, SENT), *ups,
        q_bias.reshape(1, Q_WIDTH), k_bias.reshape(1, KV_WIDTH), v_bias.reshape(1, KV_WIDTH),
        cos_table, sin_table,
    )
    ctx_parts, back, bias = attended[:4], attended[4], attended[5]
    returned = lax.all_to_all(
        back.reshape(32, 16, BACK), "col", split_axis=0, concat_axis=0, tiled=True
    )
    ctx_in = [ctx_parts[0]] + [swap(ctx_parts[s], "col", s, 32) for s in (1, 2, 3)]
    context = pl.pallas_call(
        join_kernel,
        out_shape=shape((TOK, Q_WIDTH), BF16),
        in_specs=[smem] + [vmem_spec()] * 4,
        out_specs=vmem_spec(),
        compiler_params=pltpu.CompilerParams(vmem_limit_bytes=16 * MIB),
        cost_estimate=pl.CostEstimate(flops=0, bytes_accessed=2 * MIB, transcendentals=0),
    )(col_arr, *ctx_in)

    for step in (1, 2, 4):
        bias = bias + swap(bias, "row", step, 8)
    for step in (4, 8, 16):
        bias = bias + swap(bias, "col", step, 32)
    want = row // 2
    bias = jnp.where(j == want, bias, 0.0)
    for step in (1, 2):
        bias = bias + swap(bias, "col", step, 32)
    half = lax.dynamic_slice_in_dim(bias[:8].reshape(PART), 512 * (row % 2), 512, 0)
    bias_q = lax.dynamic_slice_in_dim(half, 16 * col, 16, 0)
    bias_kv = lax.dynamic_slice_in_dim(bias[8:10], 64 * (row % 2) + 2 * col, 2, 1)

    grad_q, grad_k, grad_v = pl.pallas_call(
        unpack_kernel,
        out_shape=[shape((TOK, Q_WIDTH), BF16), shape((TOK, KV_WIDTH), BF16), shape((TOK, KV_WIDTH), BF16)],
        in_specs=[vmem_spec()] * 2,
        out_specs=[vmem_spec()] * 3,
        scratch_shapes=[
            pltpu.VMEM((TOK, PART), BF16),
            pltpu.VMEM((TOK, KV_WIDTH), BF16),
            pltpu.VMEM((TOK, KV_WIDTH), BF16),
        ],
        compiler_params=pltpu.CompilerParams(vmem_limit_bytes=24 * MIB),
        cost_estimate=pl.CostEstimate(flops=2 * 128 * 128 * 5120, bytes_accessed=4 * MIB, transcendentals=0),
    )(returned, place)
    return (context[None], grad_q[None], grad_k[None], grad_v[None], bias_q, bias_kv)


def solution(mesh):
    return jax.shard_map(
        per_device,
        mesh=mesh,
        in_specs=(
            P("row", "col", None),
            P("row", "col", None),
            P("row", "col", None),
            P(),
            P(),
            P(),
            P("row", "col"),
            P("row", "col"),
            P("row", "col", None),
        ),
        out_specs=(
            P("row", "col", None),
            P("row", "col", None),
            P("row", "col", None),
            P("row", "col", None),
            P(("row", "col")),
            P(None, ("row", "col")),
        ),
        check_vma=False,
    )
```

```python
import functools

import jax
import jax.numpy as jnp
from jax import lax
from jax.experimental import pallas as pl
from jax.experimental.pallas import tpu as pltpu
from jax.sharding import PartitionSpec as P

HEADS = 32
KV_HEADS = 4
GROUP = 8
HEAD_DIM = 128
SEGS = 8
TOK = 128
SLAB = 512
QBLK = 256
KTILE = 256
WINDOW = 1280
Q_WIDTH = HEADS * HEAD_DIM
KV_WIDTH = KV_HEADS * HEAD_DIM
PART = GROUP * HEAD_DIM
SENT = PART + 6 * HEAD_DIM + 128
BACK = PART + 6 * HEAD_DIM
MIB = 1024 * 1024

ROPE_BASE = 1000000.0
MASKED = -1e30
LOG2E = 1.4426950408889634
F32 = jnp.float32
BF16 = jnp.bfloat16

NN = (((1,), (0,)), ((), ()))
NT = (((1,), (1,)), ((), ()))


def dot(a, b, dims=NN):
    return lax.dot_general(a, b, dims, preferred_element_type=F32)


def iota(shape, axis):
    return lax.broadcasted_iota(jnp.int32, shape, axis)


def row_to_column(row, size):
    same = iota((size, size), 0) == iota((size, size), 1)
    return jnp.sum(jnp.where(same, row, 0.0), axis=1, keepdims=True)


def pack_kernel(q_hbm, k_hbm, v_hbm, place_hbm, seg_hbm, out_hbm, q_s, k_s, v_s, place_s, seg_s, out_s, sems):
    names = [(place_hbm, place_s), (seg_hbm, seg_s), (k_hbm, k_s), (v_hbm, v_s)]
    loads = [pltpu.make_async_copy(src, dst, sems.at[n]) for n, (src, dst) in enumerate(names)]
    for j in range(KV_HEADS):
        lanes = slice(PART * j, PART * (j + 1))
        loads.append(pltpu.make_async_copy(q_hbm.at[:, lanes], q_s.at[:, lanes], sems.at[4 + j]))
    for load in loads:
        load.start()
    loads[0].wait()
    loads[1].wait()
    place_row = place_s[...].astype(F32)
    place_col = row_to_column(place_row, TOK)
    rank = jnp.sum(jnp.where(place_col < place_row, 1.0, 0.0), axis=0, keepdims=True)
    pick = iota((TOK, TOK), 0).astype(F32) == rank
    pick_low = jnp.where(pick, 1.0, 0.0).astype(BF16)
    ranked = jnp.sum(jnp.where(pick, place_row, 0.0), axis=1, keepdims=True)
    inside = ranked - ((iota((TOK, 1), 0) // 16) * SLAB).astype(F32)
    high = jnp.floor(inside * (1.0 / 128.0))
    low = inside - 128.0 * high
    seg_col = row_to_column(seg_s[...].astype(F32), TOK)
    lane = iota((TOK, 128), 1)
    below = jnp.sum(
        jnp.where(seg_col < (lane - 8).astype(F32), 1.0, 0.0), axis=0, keepdims=True
    )
    lane16 = iota((16, 128), 1)
    counts = jnp.where(iota((16, 128), 0) == 0, below, 0.0)
    metas = []
    for z in range(8):
        meta = counts
        for t in range(3):
            s = (z - 2 + t) % 8
            rows = slice(16 * s, 16 * s + 16)
            meta = jnp.where(lane16 == 2 * t, high[rows], meta)
            meta = jnp.where(lane16 == 2 * t + 1, low[rows], meta)
        metas.append(meta.astype(BF16))
    loads[2].wait()
    loads[3].wait()
    keys = dot(pick_low, k_s[...]).astype(BF16)
    vals = dot(pick_low, v_s[...]).astype(BF16)
    stores = []
    for j in range(KV_HEADS):
        loads[4 + j].wait()
        part = dot(pick_low, q_s[:, PART * j : PART * (j + 1)]).astype(BF16)
        head = slice(HEAD_DIM * j, HEAD_DIM * (j + 1))
        for z in range(8):
            out_s[z, j, :, 0:PART] = part[16 * z : 16 * z + 16]
            for t in range(3):
                s = (z - 2 + t) % 8
                rows = slice(16 * s, 16 * s + 16)
                base = PART + 256 * t
                out_s[z, j, :, base : base + 128] = keys[rows, head]
                out_s[z, j, :, base + 128 : base + 256] = vals[rows, head]
            out_s[z, j, :, BACK:SENT] = metas[z]
        store = pltpu.make_async_copy(out_s.at[:, j], out_hbm.at[:, j], sems.at[8 + j])
        store.start()
        stores.append(store)
    for store in stores:
        store.wait()


def turn(values, cosine, sine):
    return values * cosine + pltpu.roll(values, HEAD_DIM // 2, 1) * sine


def unturn(values, cosine, sine):
    return values * cosine - pltpu.roll(values, HEAD_DIM // 2, 1) * sine


def attend_kernel(
    col_ref, recv_hbm, up0, up1, up2, up3, qb_hbm, kb_hbm, vb_hbm, cos_hbm, sin_hbm,
    ctx0, ctx1, ctx2, ctx3, back_hbm, bias_ref,
    recv_s, cos_t, sin_t, qb_s, kb_s, vb_s,
    up_s, q_s, k_s, v_s, kt_s, vt_s, cos_s, sin_s, mask_s, s_s, p_s, dk_s, dv_s, ctx_s, dq_s, back_s, sems,
):
    col = col_ref[0]
    z = col // 4
    j = col % 4
    first = SLAB * (z - 2)
    scale = HEAD_DIM ** (-0.5)

    copies = [
        pltpu.make_async_copy(recv_hbm, recv_s, sems.at[0]),
        pltpu.make_async_copy(cos_hbm, cos_t, sems.at[1]),
        pltpu.make_async_copy(sin_hbm, sin_t, sems.at[2]),
        pltpu.make_async_copy(kb_hbm.at[:, pl.ds(pl.multiple_of(HEAD_DIM * j, HEAD_DIM), HEAD_DIM)], kb_s, sems.at[3]),
        pltpu.make_async_copy(vb_hbm.at[:, pl.ds(pl.multiple_of(HEAD_DIM * j, HEAD_DIM), HEAD_DIM)], vb_s, sems.at[4]),
        pltpu.make_async_copy(qb_hbm.at[:, pl.ds(pl.multiple_of(PART * j, PART), PART)], qb_s, sems.at[5]),
    ]
    for s, ref in enumerate((up0, up1, up2, up3)):
        copies.append(
            pltpu.make_async_copy(
                ref, up_s.at[pl.ds(pl.multiple_of(TOK * (j ^ s), TOK), TOK), :], sems.at[6 + s]
            )
        )
    for copy in copies:
        copy.start()
    dk_s[...] = jnp.zeros_like(dk_s)
    dv_s[...] = jnp.zeros_like(dv_s)
    cos_s[...] = jnp.zeros_like(cos_s)
    sin_s[...] = jnp.zeros_like(sin_s)
    mask_s[...] = jnp.where(iota((QBLK, QBLK), 0) <= iota((QBLK, QBLK), 1), 0.0, MASKED)
    for copy in copies:
        copy.wait()

    meta = recv_s[:, BACK:SENT].astype(F32)
    meta_rows = jnp.transpose(meta)
    sums = jnp.sum(meta, axis=0, keepdims=True)
    starts = [jnp.sum(meta[:, 8 + v : 9 + v]).astype(jnp.int32) for v in range(SEGS)]

    for b in range(12):
        at = first + TOK * b
        rows = slice(TOK * b, TOK * (b + 1))
        for v in range(SEGS):
            begin = starts[v]
            end = starts[v + 1] if v + 1 < SEGS else jnp.int32(8 * SLAB)

            @pl.when((begin < at + TOK) & (end > at))
            def _():
                src = pl.ds(at - begin + TOK, TOK)
                inside = at + iota((TOK, HEAD_DIM), 0) >= begin
                cos_s[rows, :] = jnp.where(inside, cos_t[src, :], cos_s[rows, :])
                sin_s[rows, :] = jnp.where(inside, sin_t[src, :], sin_s[rows, :])

    lane = iota((1, HEAD_DIM), 1)
    named = (lane >= 8) & (lane < 16)
    lower = jnp.where(named, sums, 1e9)
    upper = jnp.where(named, jnp.where(lane == 15, 8.0 * SLAB, pltpu.roll(sums, HEAD_DIM - 1, 1)), -1e9)
    upper = jnp.where(lane == 16, 0.0, upper)
    lower = jnp.where(lane == 16, -1e9, lower)
    spot = iota((SLAB, SLAB), 0).astype(F32)
    for t in range(3):
        pos = meta_rows[2 * t : 2 * t + 1] * 128.0 + meta_rows[2 * t + 1 : 2 * t + 2]
        pick = jnp.where(spot == pos, 1.0, 0.0).astype(BF16)
        rows = slice(SLAB * t, SLAB * (t + 1))
        base = PART + 256 * t
        both = dot(pick, recv_s[:, base : base + 256])
        keys = turn(both[:, :128] + kb_s[...], cos_s[rows, :], sin_s[rows, :])
        vals = both[:, 128:] + vb_s[...]
        at = (first + SLAB * t + iota((SLAB, HEAD_DIM), 0)).astype(F32)
        name = jnp.where((at >= lower) & (at < upper), 1.0, 0.0)
        k_s[rows, 0:HEAD_DIM] = keys.astype(BF16)
        k_s[rows, HEAD_DIM:] = name.astype(BF16)
        v_s[rows, :] = vals.astype(BF16)
        kt_s[:, rows] = jnp.transpose(keys).astype(BF16)
        vt_s[:, rows] = jnp.transpose(vals).astype(BF16)
        if t == 2:
            other = jnp.where((lane >= 8) & (lane < 17), MASKED * (1.0 - name), 0.0).astype(BF16)
            for pair in range(4):
                lanes = slice(256 * pair, 256 * (pair + 1))
                both = dot(pick, recv_s[:, lanes]) + qb_s[:, lanes]
                for u in range(2):
                    one = both[:, 128 * u : 128 * (u + 1)]
                    q_s[2 * pair + u, :, 0:HEAD_DIM] = turn(one, cos_s[rows, :], sin_s[rows, :]).astype(BF16)
                    q_s[2 * pair + u, :, HEAD_DIM:] = other

    def one_head(h, _):
        lanes = pl.ds(pl.multiple_of(h * HEAD_DIM, HEAD_DIM), HEAD_DIM)
        blocks = range(2)
        q_rows = [slice(QBLK * i, QBLK * (i + 1)) for i in blocks]
        k_rows = [slice(QBLK * i, QBLK * i + WINDOW) for i in blocks]
        query = [q_s[h, q_rows[i], 0:HEAD_DIM] for i in blocks]
        up = [up_s[q_rows[i], lanes] for i in blocks]
        up_t = [jnp.transpose(up[i].astype(F32)) for i in blocks]
        top = [None, None]
        invert = [None, None]
        out_low = [None, None]
        dq_t = [None, None]
        for i in blocks:
            score = dot(k_s[k_rows[i], :], q_s[h, q_rows[i], :], NT)
            s_s[i, 0 : WINDOW - QBLK, :] = score[: WINDOW - QBLK]
            last = score[WINDOW - QBLK :] + mask_s[...]
            s_s[i, WINDOW - QBLK :, :] = last
            top[i] = jnp.maximum(
                jnp.max(score[: WINDOW - QBLK], axis=0, keepdims=True), jnp.max(last, axis=0, keepdims=True)
            )
        for i in blocks:
            p_s[i] = dot(v_s[k_rows[i], :], up[i], NT)
        for i in blocks:
            weight = jnp.exp2((s_s[i] - top[i]) * (scale * LOG2E))
            s_s[i] = weight
            invert[i] = 1.0 / jnp.sum(weight, axis=0, keepdims=True)
        for i in blocks:
            prob = s_s[i] * invert[i]
            s_s[i] = prob
            prob_low = prob.astype(BF16)
            out_t = dot(vt_s[:, k_rows[i]], prob_low)
            dv_s[k_rows[i], :] += dot(prob_low, up[i])
            out_low[i] = out_t.astype(BF16).astype(F32)
        for i in blocks:
            ctx_s[q_rows[i], lanes] = jnp.transpose(out_low[i]).astype(BF16)
            delta = jnp.sum(up_t[i] * out_low[i], axis=0, keepdims=True)
            dscore = (s_s[i] * (p_s[i] - delta)).astype(BF16)
            dq_t[i] = dot(kt_s[:, k_rows[i]], dscore)
            dk_s[k_rows[i], :] += dot(dscore, query[i])
        total = None
        for i in blocks:
            dq = jnp.transpose(dq_t[i]) * scale
            w_rows = slice(2 * SLAB + QBLK * i, 2 * SLAB + QBLK * (i + 1))
            dq = unturn(dq, cos_s[w_rows, :], sin_s[w_rows, :])
            dq_s[q_rows[i], lanes] = dq.astype(BF16)
            mine = jnp.sum(dq, axis=0, keepdims=True)
            total = mine if total is None else total + mine
        bias_ref[pl.ds(h, 1), :] = total
        return 0

    lax.fori_loop(0, GROUP, one_head, 0, unroll=2)

    outs = []
    for s, ref in enumerate((ctx0, ctx1, ctx2, ctx3)):
        outs.append(
            pltpu.make_async_copy(
                ctx_s.at[pl.ds(pl.multiple_of(TOK * (j ^ s), TOK), TOK), :], ref, sems.at[6 + s]
            )
        )
    for copy in outs:
        copy.start()

    sum_k = jnp.zeros((1, HEAD_DIM), F32)
    sum_v = jnp.zeros((1, HEAD_DIM), F32)
    across = iota((SLAB, SLAB), 1).astype(F32)
    for t in (2, 0, 1):
        rows = slice(SLAB * t, SLAB * (t + 1))
        pos = meta[:, 2 * t : 2 * t + 1] * 128.0 + meta[:, 2 * t + 1 : 2 * t + 2]
        drop = jnp.where(across == pos, 1.0, 0.0).astype(BF16)
        if t == 2:
            back_s[:, 0:PART] = dot(drop, dq_s[...]).astype(BF16)
            main = pltpu.make_async_copy(back_s.at[:, 0:PART], back_hbm.at[:, 0:PART], sems.at[0])
            main.start()
            outs.append(main)
        dk = unturn(dk_s[rows, :] * scale, cos_s[rows, :], sin_s[rows, :])
        dv = dv_s[rows, :]
        sum_k = sum_k + jnp.sum(dk, axis=0, keepdims=True)
        sum_v = sum_v + jnp.sum(dv, axis=0, keepdims=True)
        base = PART + 256 * t
        both = jnp.concatenate([dk.astype(BF16), dv.astype(BF16)], axis=1)
        back_s[:, base : base + 256] = dot(drop, both).astype(BF16)
        side = pltpu.make_async_copy(back_s.at[:, base : base + 256], back_hbm.at[:, base : base + 256], sems.at[1 + t])
        side.start()
        outs.append(side)
    bias_ref[8:9, :] = sum_k
    bias_ref[9:10, :] = sum_v
    bias_ref[10:16, :] = jnp.zeros((6, HEAD_DIM), F32)
    for copy in outs:
        copy.wait()


def join_kernel(col_ref, c0, c1, c2, c3, out_ref):
    j = col_ref[0] % 4
    for s, ref in enumerate((c0, c1, c2, c3)):
        out_ref[:, pl.ds(pl.multiple_of(PART * (j ^ s), PART), PART)] = ref[...]


def finish_kernel(at_ref, mine_ref, other_ref, q_ref, kv_ref):
    col = at_ref[0]
    half = at_ref[1] % 2
    total = mine_ref[...] + other_ref[...]
    line = jnp.sum(
        jnp.where(iota((16, 128), 0) == 4 * half + col // 8, total, 0.0), axis=0, keepdims=True
    )
    q_ref[...] = pltpu.roll(line, (128 - 16 * (col % 8)) % 128, 1)[:, :16]
    kv_ref[...] = pltpu.roll(total[8:16], (128 - 64 * half - 2 * col) % 128, 1)[:2, :2]


def unpack_kernel(back_ref, place_ref, gq_ref, gk_ref, gv_ref, q_s, k_s, v_s):
    place_row = place_ref[...].astype(F32)
    place_col = row_to_column(place_row, TOK)
    rank = jnp.sum(jnp.where(place_row < place_col, 1.0, 0.0), axis=1, keepdims=True)
    pick = jnp.where(iota((TOK, TOK), 1).astype(F32) == rank, 1.0, 0.0).astype(BF16)
    for j in range(KV_HEADS):
        head = slice(HEAD_DIM * j, HEAD_DIM * (j + 1))
        for s in range(8):
            rows = slice(16 * s, 16 * s + 16)
            q_s[rows, :] = back_ref[4 * s + j, :, 0:PART]
            total = None
            for t in range(3):
                base = PART + 256 * t
                term = back_ref[4 * ((s + 2 - t) % 8) + j, :, base : base + 256].astype(F32)
                total = term if total is None else total + term
            k_s[rows, head] = total[:, :128].astype(BF16)
            v_s[rows, head] = total[:, 128:].astype(BF16)
        gq_ref[:, PART * j : PART * (j + 1)] = dot(pick, q_s[...]).astype(BF16)
    gk_ref[...] = dot(pick, k_s[...]).astype(BF16)
    gv_ref[...] = dot(pick, v_s[...]).astype(BF16)


def any_spec():
    return pl.BlockSpec(memory_space=pltpu.HBM)


def vmem_spec():
    return pl.BlockSpec(memory_space=pltpu.VMEM)


def shape(dims, dtype):
    return jax.ShapeDtypeStruct(dims, dtype)


def swap(values, axis, step, size):
    return lax.ppermute(values, axis, [(c, c ^ step) for c in range(size)])


def rotation_tables():
    offset = jnp.arange(-TOK, 1024 + TOK, dtype=jnp.int32).astype(F32)
    powers = jnp.arange(HEAD_DIM // 2, dtype=F32) * (2.0 / HEAD_DIM)
    rates = ROPE_BASE ** (-powers)
    angle = offset[:, None] * rates[None, :]
    cosine = jnp.cos(angle)
    sine = jnp.sin(angle)
    return (
        jnp.concatenate([cosine, cosine], axis=1),
        jnp.concatenate([-sine, sine], axis=1),
    )


def attend(col_arr, recv, ups, q_bias, k_bias, v_bias):
    cos_table, sin_table = rotation_tables()
    return pl.pallas_call(
        attend_kernel,
        out_shape=[shape((TOK, PART), BF16)] * 4
        + [shape((SLAB, BACK), BF16), shape((16, HEAD_DIM), F32)],
        in_specs=[pl.BlockSpec(memory_space=pltpu.SMEM)] + [any_spec()] * 10,
        out_specs=[any_spec()] * 5 + [vmem_spec()],
        scratch_shapes=[
            pltpu.VMEM((SLAB, SENT), BF16),
            pltpu.VMEM((1280, HEAD_DIM), F32),
            pltpu.VMEM((1280, HEAD_DIM), F32),
            pltpu.VMEM((1, PART), F32),
            pltpu.VMEM((1, HEAD_DIM), F32),
            pltpu.VMEM((1, HEAD_DIM), F32),
            pltpu.VMEM((SLAB, PART), BF16),
            pltpu.VMEM((GROUP, SLAB, 2 * HEAD_DIM), BF16),
            pltpu.VMEM((3 * SLAB, 2 * HEAD_DIM), BF16),
            pltpu.VMEM((3 * SLAB, HEAD_DIM), BF16),
            pltpu.VMEM((HEAD_DIM, 3 * SLAB), BF16),
            pltpu.VMEM((HEAD_DIM, 3 * SLAB), BF16),
            pltpu.VMEM((3 * SLAB, HEAD_DIM), F32),
            pltpu.VMEM((3 * SLAB, HEAD_DIM), F32),
            pltpu.VMEM((QBLK, QBLK), F32),
            pltpu.VMEM((2, WINDOW, QBLK), F32),
            pltpu.VMEM((2, WINDOW, QBLK), F32),
            pltpu.VMEM((3 * SLAB, HEAD_DIM), F32),
            pltpu.VMEM((3 * SLAB, HEAD_DIM), F32),
            pltpu.VMEM((SLAB, PART), BF16),
            pltpu.VMEM((SLAB, PART), BF16),
            pltpu.VMEM((SLAB, BACK), BF16),
            pltpu.SemaphoreType.DMA((10,)),
        ],
        compiler_params=pltpu.CompilerParams(vmem_limit_bytes=60 * MIB),
        cost_estimate=pl.CostEstimate(flops=8 * 10**9, bytes_accessed=8 * MIB, transcendentals=5 * 10**6),
    )(col_arr, recv, *ups, q_bias, k_bias, v_bias, cos_table, sin_table)


def per_device(q_load, k_load, v_load, q_bias, k_bias, v_bias, place, segment, d_context):
    col = lax.axis_index("col")
    row = lax.axis_index("row")
    j = col % 4
    col_arr = col.reshape(1).astype(jnp.int32)
    smem = pl.BlockSpec(memory_space=pltpu.SMEM)

    packed = pl.pallas_call(
        pack_kernel,
        out_shape=shape((8, KV_HEADS, 16, SENT), BF16),
        in_specs=[any_spec()] * 5,
        out_specs=any_spec(),
        scratch_shapes=[
            pltpu.VMEM((TOK, Q_WIDTH), BF16),
            pltpu.VMEM((TOK, KV_WIDTH), BF16),
            pltpu.VMEM((TOK, KV_WIDTH), BF16),
            pltpu.VMEM((1, TOK), jnp.int32),
            pltpu.VMEM((1, TOK), jnp.int32),
            pltpu.VMEM((8, KV_HEADS, 16, SENT), BF16),
            pltpu.SemaphoreType.DMA((12,)),
        ],
        compiler_params=pltpu.CompilerParams(vmem_limit_bytes=60 * MIB),
        cost_estimate=pl.CostEstimate(flops=2 * 128 * 128 * 5120, bytes_accessed=5 * MIB, transcendentals=0),
    )(q_load[0], k_load[0], v_load[0], place, segment)
    recv = lax.all_to_all(
        packed.reshape(32, 16, SENT), "col", split_axis=0, concat_axis=0, tiled=True
    )

    up_own = d_context[0]
    ups = []
    for s in range(4):
        piece = lax.dynamic_slice_in_dim(up_own, PART * (j ^ s), PART, 1)
        ups.append(piece if s == 0 else swap(piece, "col", s, 32))
    attended = attend(
        col_arr, recv.reshape(SLAB, SENT), ups,
        q_bias.reshape(1, Q_WIDTH), k_bias.reshape(1, KV_WIDTH), v_bias.reshape(1, KV_WIDTH),
    )
    ctx_parts, back, bias = attended[:4], attended[4], attended[5]
    returned = lax.all_to_all(
        back.reshape(32, 16, BACK), "col", split_axis=0, concat_axis=0, tiled=True
    )
    ctx_in = [ctx_parts[0], swap(ctx_parts[1], "col", 1, 32)]
    ctx_in += [swap(ctx_parts[2], "col", 2, 32), swap(ctx_parts[3], "col", 3, 32)]
    for step in (2, 4):
        bias = bias + swap(bias, "row", step, 8)
    bias, ctx_in[2], ctx_in[3] = lax.optimization_barrier((bias, ctx_in[2], ctx_in[3]))
    context = pl.pallas_call(
        join_kernel,
        out_shape=shape((TOK, Q_WIDTH), BF16),
        in_specs=[smem] + [vmem_spec()] * 4,
        out_specs=vmem_spec(),
        compiler_params=pltpu.CompilerParams(vmem_limit_bytes=16 * MIB),
        cost_estimate=pl.CostEstimate(flops=0, bytes_accessed=2 * MIB, transcendentals=0),
    )(col_arr, *ctx_in)
    bias = bias + swap(bias, "row", 1, 8)
    bias = jnp.where(j == row // 2, bias, 0.0)
    for step in (1, 2):
        bias = bias + swap(bias, "col", step, 32)
    bias = bias + (swap(bias, "col", 8, 32) + swap(bias, "col", 16, 32) + swap(bias, "col", 24, 32))
    other = swap(bias, "col", 4, 32)
    bias_q, bias_kv = pl.pallas_call(
        finish_kernel,
        out_shape=[shape((1, 16), F32), shape((2, 2), F32)],
        in_specs=[smem, vmem_spec(), vmem_spec()],
        out_specs=[vmem_spec()] * 2,
        compiler_params=pltpu.CompilerParams(vmem_limit_bytes=8 * MIB),
        cost_estimate=pl.CostEstimate(flops=0, bytes_accessed=32768, transcendentals=0),
    )(jnp.stack([col, row]).astype(jnp.int32), bias, other)
    bias_q = bias_q.reshape(16)

    grad_q, grad_k, grad_v = pl.pallas_call(
        unpack_kernel,
        out_shape=[shape((TOK, Q_WIDTH), BF16), shape((TOK, KV_WIDTH), BF16), shape((TOK, KV_WIDTH), BF16)],
        in_specs=[vmem_spec()] * 2,
        out_specs=[vmem_spec()] * 3,
        scratch_shapes=[
            pltpu.VMEM((TOK, PART), BF16),
            pltpu.VMEM((TOK, KV_WIDTH), BF16),
            pltpu.VMEM((TOK, KV_WIDTH), BF16),
        ],
        compiler_params=pltpu.CompilerParams(vmem_limit_bytes=24 * MIB),
        cost_estimate=pl.CostEstimate(flops=2 * 128 * 128 * 5120, bytes_accessed=4 * MIB, transcendentals=0),
    )(returned, place)
    return (context[None], grad_q[None], grad_k[None], grad_v[None], bias_q, bias_kv)


def solution(mesh):
    return jax.shard_map(
        per_device,
        mesh=mesh,
        in_specs=(
            P("row", "col", None),
            P("row", "col", None),
            P("row", "col", None),
            P(),
            P(),
            P(),
            P("row", "col"),
            P("row", "col"),
            P("row", "col", None),
        ),
        out_specs=(
            P("row", "col", None),
            P("row", "col", None),
            P("row", "col", None),
            P("row", "col", None),
            P(("row", "col")),
            P(None, ("row", "col")),
        ),
        check_vma=False,
    )
```

```python
import functools

import jax
import jax.numpy as jnp
from jax import lax
from jax.experimental import pallas as pl
from jax.experimental.pallas import tpu as pltpu
from jax.sharding import PartitionSpec as P

HEADS = 32
KV_HEADS = 4
GROUP = 8
HEAD_DIM = 128
SEGS = 8
TOK = 128
SLAB = 512
QBLK = 256
KTILE = 256
WINDOW = 1280
Q_WIDTH = HEADS * HEAD_DIM
KV_WIDTH = KV_HEADS * HEAD_DIM
PART = GROUP * HEAD_DIM
SENT = PART + 6 * HEAD_DIM + 128
BACK = PART + 6 * HEAD_DIM
MIB = 1024 * 1024

ROPE_BASE = 1000000.0
MASKED = -1e30
LOG2E = 1.4426950408889634
F32 = jnp.float32
BF16 = jnp.bfloat16

NN = (((1,), (0,)), ((), ()))
NT = (((1,), (1,)), ((), ()))


def dot(a, b, dims=NN):
    return lax.dot_general(a, b, dims, preferred_element_type=F32)


def iota(shape, axis):
    return lax.broadcasted_iota(jnp.int32, shape, axis)


def row_to_column(row, size):
    same = iota((size, size), 0) == iota((size, size), 1)
    return jnp.sum(jnp.where(same, row, 0.0), axis=1, keepdims=True)


def pack_kernel(q_hbm, k_hbm, v_hbm, place_hbm, seg_hbm, out_hbm, q_s, k_s, v_s, place_s, seg_s, out_s, sems):
    names = [(place_hbm, place_s), (seg_hbm, seg_s), (k_hbm, k_s), (v_hbm, v_s)]
    loads = [pltpu.make_async_copy(src, dst, sems.at[n]) for n, (src, dst) in enumerate(names)]
    for j in range(KV_HEADS):
        lanes = slice(PART * j, PART * (j + 1))
        loads.append(pltpu.make_async_copy(q_hbm.at[:, lanes], q_s.at[:, lanes], sems.at[4 + j]))
    for load in loads:
        load.start()
    loads[0].wait()
    loads[1].wait()
    place_row = place_s[...].astype(F32)
    place_col = row_to_column(place_row, TOK)
    rank = jnp.sum(jnp.where(place_col < place_row, 1.0, 0.0), axis=0, keepdims=True)
    pick = iota((TOK, TOK), 0).astype(F32) == rank
    pick_low = jnp.where(pick, 1.0, 0.0).astype(BF16)
    ranked = jnp.sum(jnp.where(pick, place_row, 0.0), axis=1, keepdims=True)
    inside = ranked - ((iota((TOK, 1), 0) // 16) * SLAB).astype(F32)
    high = jnp.floor(inside * (1.0 / 128.0))
    low = inside - 128.0 * high
    seg_col = row_to_column(seg_s[...].astype(F32), TOK)
    lane = iota((TOK, 128), 1)
    below = jnp.sum(
        jnp.where(seg_col < (lane - 8).astype(F32), 1.0, 0.0), axis=0, keepdims=True
    )
    lane16 = iota((16, 128), 1)
    counts = jnp.where(iota((16, 128), 0) == 0, below, 0.0)
    metas = []
    for z in range(8):
        meta = counts
        for t in range(3):
            s = (z - 2 + t) % 8
            rows = slice(16 * s, 16 * s + 16)
            meta = jnp.where(lane16 == 2 * t, high[rows], meta)
            meta = jnp.where(lane16 == 2 * t + 1, low[rows], meta)
        metas.append(meta.astype(BF16))
    loads[2].wait()
    loads[3].wait()
    keys = dot(pick_low, k_s[...]).astype(BF16)
    vals = dot(pick_low, v_s[...]).astype(BF16)
    stores = []
    for j in range(KV_HEADS):
        loads[4 + j].wait()
        part = dot(pick_low, q_s[:, PART * j : PART * (j + 1)]).astype(BF16)
        head = slice(HEAD_DIM * j, HEAD_DIM * (j + 1))
        for z in range(8):
            out_s[z, j, :, 0:PART] = part[16 * z : 16 * z + 16]
            for t in range(3):
                s = (z - 2 + t) % 8
                rows = slice(16 * s, 16 * s + 16)
                base = PART + 256 * t
                out_s[z, j, :, base : base + 128] = keys[rows, head]
                out_s[z, j, :, base + 128 : base + 256] = vals[rows, head]
            out_s[z, j, :, BACK:SENT] = metas[z]
        store = pltpu.make_async_copy(out_s.at[:, j], out_hbm.at[:, j], sems.at[8 + j])
        store.start()
        stores.append(store)
    for store in stores:
        store.wait()


def turn(values, cosine, sine):
    return values * cosine + pltpu.roll(values, HEAD_DIM // 2, 1) * sine


def unturn(values, cosine, sine):
    return values * cosine - pltpu.roll(values, HEAD_DIM // 2, 1) * sine


def attend_kernel(
    col_ref, recv_hbm, up0, up1, up2, up3, qb_hbm, kb_hbm, vb_hbm, cos_hbm, sin_hbm,
    ctx0, ctx1, ctx2, ctx3, back_hbm, bias_ref,
    recv_s, cos_t, sin_t, qb_s, kb_s, vb_s,
    up_s, q_s, k_s, v_s, kt_s, vt_s, cos_s, sin_s, mask_s, s_s, p_s, dk_s, dv_s, ctx_s, dq_s, back_s, sems,
):
    col = col_ref[0]
    z = col // 4
    j = col % 4
    first = SLAB * (z - 2)
    scale = HEAD_DIM ** (-0.5)

    copies = [
        pltpu.make_async_copy(recv_hbm, recv_s, sems.at[0]),
        pltpu.make_async_copy(cos_hbm, cos_t, sems.at[1]),
        pltpu.make_async_copy(sin_hbm, sin_t, sems.at[2]),
        pltpu.make_async_copy(kb_hbm.at[:, pl.ds(pl.multiple_of(HEAD_DIM * j, HEAD_DIM), HEAD_DIM)], kb_s, sems.at[3]),
        pltpu.make_async_copy(vb_hbm.at[:, pl.ds(pl.multiple_of(HEAD_DIM * j, HEAD_DIM), HEAD_DIM)], vb_s, sems.at[4]),
        pltpu.make_async_copy(qb_hbm.at[:, pl.ds(pl.multiple_of(PART * j, PART), PART)], qb_s, sems.at[5]),
    ]
    for s, ref in enumerate((up0, up1, up2, up3)):
        copies.append(
            pltpu.make_async_copy(
                ref, up_s.at[pl.ds(pl.multiple_of(TOK * (j ^ s), TOK), TOK), :], sems.at[6 + s]
            )
        )
    for copy in copies:
        copy.start()
    dk_s[...] = jnp.zeros_like(dk_s)
    dv_s[...] = jnp.zeros_like(dv_s)
    cos_s[...] = jnp.zeros_like(cos_s)
    sin_s[...] = jnp.zeros_like(sin_s)
    mask_s[...] = jnp.where(iota((QBLK, QBLK), 0) <= iota((QBLK, QBLK), 1), 0.0, MASKED)
    for copy in copies[:6]:
        copy.wait()

    meta = recv_s[:, BACK:SENT].astype(F32)
    meta_rows = jnp.transpose(meta)
    sums = jnp.sum(meta, axis=0, keepdims=True)
    starts = [jnp.sum(meta[:, 8 + v : 9 + v]).astype(jnp.int32) for v in range(SEGS)]

    for b in range(12):
        at = first + TOK * b
        rows = slice(TOK * b, TOK * (b + 1))
        for v in range(SEGS):
            begin = starts[v]
            end = starts[v + 1] if v + 1 < SEGS else jnp.int32(8 * SLAB)

            @pl.when((begin < at + TOK) & (end > at))
            def _():
                src = pl.ds(at - begin + TOK, TOK)
                inside = at + iota((TOK, HEAD_DIM), 0) >= begin
                cos_s[rows, :] = jnp.where(inside, cos_t[src, :], cos_s[rows, :])
                sin_s[rows, :] = jnp.where(inside, sin_t[src, :], sin_s[rows, :])

    lane = iota((1, HEAD_DIM), 1)
    named = (lane >= 8) & (lane < 16)
    lower = jnp.where(named, sums, 1e9)
    upper = jnp.where(named, jnp.where(lane == 15, 8.0 * SLAB, pltpu.roll(sums, HEAD_DIM - 1, 1)), -1e9)
    upper = jnp.where(lane == 16, 0.0, upper)
    lower = jnp.where(lane == 16, -1e9, lower)
    spot = iota((SLAB, SLAB), 0).astype(F32)
    for t in range(3):
        pos = meta_rows[2 * t : 2 * t + 1] * 128.0 + meta_rows[2 * t + 1 : 2 * t + 2]
        pick = jnp.where(spot == pos, 1.0, 0.0).astype(BF16)
        rows = slice(SLAB * t, SLAB * (t + 1))
        base = PART + 256 * t
        both = dot(pick, recv_s[:, base : base + 256])
        keys = turn(both[:, :128] + kb_s[...], cos_s[rows, :], sin_s[rows, :])
        vals = both[:, 128:] + vb_s[...]
        at = (first + SLAB * t + iota((SLAB, HEAD_DIM), 0)).astype(F32)
        name = jnp.where((at >= lower) & (at < upper), 1.0, 0.0)
        k_s[rows, 0:HEAD_DIM] = keys.astype(BF16)
        k_s[rows, HEAD_DIM:] = name.astype(BF16)
        v_s[rows, :] = vals.astype(BF16)
        kt_s[:, rows] = jnp.transpose(keys).astype(BF16)
        vt_s[:, rows] = jnp.transpose(vals).astype(BF16)
        if t == 2:
            other = jnp.where((lane >= 8) & (lane < 17), MASKED * (1.0 - name), 0.0).astype(BF16)
            for pair in range(4):
                lanes = slice(256 * pair, 256 * (pair + 1))
                both = dot(pick, recv_s[:, lanes]) + qb_s[:, lanes]
                for u in range(2):
                    one = both[:, 128 * u : 128 * (u + 1)]
                    q_s[2 * pair + u, :, 0:HEAD_DIM] = turn(one, cos_s[rows, :], sin_s[rows, :]).astype(BF16)
                    q_s[2 * pair + u, :, HEAD_DIM:] = other

    for copy in copies[6:]:
        copy.wait()

    def one_head(h, spans):
        lanes = pl.ds(pl.multiple_of(h * HEAD_DIM, HEAD_DIM), HEAD_DIM)
        blocks = range(2)
        q_rows = [slice(QBLK * i, QBLK * (i + 1)) for i in blocks]
        k_rows = [slice(begin, begin + size) for begin, size in spans]
        size = [span[1] for span in spans]
        query = [q_s[h, q_rows[i], 0:HEAD_DIM] for i in blocks]
        up = [up_s[q_rows[i], lanes] for i in blocks]
        up_t = [jnp.transpose(up[i].astype(F32)) for i in blocks]
        top = [None, None]
        invert = [None, None]
        out_low = [None, None]
        dq_t = [None, None]
        for i in blocks:
            edge = size[i] - QBLK
            score = dot(k_s[k_rows[i], :], q_s[h, q_rows[i], :], NT)
            s_s[i, 0:edge, :] = score[:edge]
            last = score[edge:] + mask_s[...]
            s_s[i, edge : size[i], :] = last
            top[i] = jnp.maximum(
                jnp.max(score[:edge], axis=0, keepdims=True), jnp.max(last, axis=0, keepdims=True)
            )
        for i in blocks:
            p_s[i, 0 : size[i], :] = dot(v_s[k_rows[i], :], up[i], NT)
        for i in blocks:
            weight = jnp.exp2((s_s[i, 0 : size[i], :] - top[i]) * (scale * LOG2E))
            s_s[i, 0 : size[i], :] = weight
            invert[i] = 1.0 / jnp.sum(weight, axis=0, keepdims=True)
        for i in blocks:
            prob_low = (s_s[i, 0 : size[i], :] * invert[i]).astype(BF16)
            out_t = dot(vt_s[:, k_rows[i]], prob_low)
            dv_s[k_rows[i], :] += dot(prob_low, up[i])
            out_low[i] = out_t.astype(BF16).astype(F32)
        for i in blocks:
            ctx_s[q_rows[i], lanes] = jnp.transpose(out_low[i]).astype(BF16)
            delta = jnp.sum(up_t[i] * out_low[i], axis=0, keepdims=True)
            prob = s_s[i, 0 : size[i], :] * invert[i]
            dscore = (prob * (p_s[i, 0 : size[i], :] - delta)).astype(BF16)
            dq_t[i] = dot(kt_s[:, k_rows[i]], dscore)
            dk_s[k_rows[i], :] += dot(dscore, query[i])
        total = None
        for i in blocks:
            dq = jnp.transpose(dq_t[i]) * scale
            w_rows = slice(2 * SLAB + QBLK * i, 2 * SLAB + QBLK * (i + 1))
            dq = unturn(dq, cos_s[w_rows, :], sin_s[w_rows, :])
            dq_s[q_rows[i], lanes] = dq.astype(BF16)
            mine = jnp.sum(dq, axis=0, keepdims=True)
            total = mine if total is None else total + mine
        bias_ref[pl.ds(h, 1), :] = total

    def all_heads(spans):
        def step(h, _):
            one_head(h, spans)
            return 0

        lax.fori_loop(0, GROUP, step, 0, unroll=2)

    middle = SLAB * z + QBLK
    begin = jnp.int32(0)
    for v in range(1, SEGS):
        begin = jnp.where(starts[v] <= middle, starts[v], begin)
    far = begin < middle - (WINDOW - 2 * QBLK)

    @pl.when(far)
    def _():
        all_heads(((QBLK, WINDOW - QBLK), (QBLK, WINDOW)))

    @pl.when(jnp.logical_not(far))
    def _():
        all_heads(((0, WINDOW), (2 * QBLK, WINDOW - QBLK)))

    outs = []
    for s, ref in enumerate((ctx0, ctx1, ctx2, ctx3)):
        outs.append(
            pltpu.make_async_copy(
                ctx_s.at[pl.ds(pl.multiple_of(TOK * (j ^ s), TOK), TOK), :], ref, sems.at[6 + s]
            )
        )
    for copy in outs:
        copy.start()

    sum_k = jnp.zeros((1, HEAD_DIM), F32)
    sum_v = jnp.zeros((1, HEAD_DIM), F32)
    across = iota((SLAB, SLAB), 1).astype(F32)
    for t in (2, 0, 1):
        rows = slice(SLAB * t, SLAB * (t + 1))
        pos = meta[:, 2 * t : 2 * t + 1] * 128.0 + meta[:, 2 * t + 1 : 2 * t + 2]
        drop = jnp.where(across == pos, 1.0, 0.0).astype(BF16)
        if t == 2:
            back_s[:, 0:PART] = dot(drop, dq_s[...]).astype(BF16)
            main = pltpu.make_async_copy(back_s.at[:, 0:PART], back_hbm.at[:, 0:PART], sems.at[0])
            main.start()
            outs.append(main)
        dk = unturn(dk_s[rows, :] * scale, cos_s[rows, :], sin_s[rows, :])
        dv = dv_s[rows, :]
        sum_k = sum_k + jnp.sum(dk, axis=0, keepdims=True)
        sum_v = sum_v + jnp.sum(dv, axis=0, keepdims=True)
        base = PART + 256 * t
        both = jnp.concatenate([dk.astype(BF16), dv.astype(BF16)], axis=1)
        back_s[:, base : base + 256] = dot(drop, both).astype(BF16)
        side = pltpu.make_async_copy(back_s.at[:, base : base + 256], back_hbm.at[:, base : base + 256], sems.at[1 + t])
        side.start()
        outs.append(side)
    bias_ref[8:9, :] = sum_k
    bias_ref[9:10, :] = sum_v
    bias_ref[10:16, :] = jnp.zeros((6, HEAD_DIM), F32)
    for copy in outs:
        copy.wait()


def join_kernel(col_ref, c0, c1, c2, c3, out_ref):
    j = col_ref[0] % 4
    for s, ref in enumerate((c0, c1, c2, c3)):
        out_ref[:, pl.ds(pl.multiple_of(PART * (j ^ s), PART), PART)] = ref[...]


def finish_kernel(at_ref, mine_ref, other_ref, q_ref, kv_ref):
    col = at_ref[0]
    half = at_ref[1] % 2
    total = mine_ref[...] + other_ref[...]
    line = jnp.sum(
        jnp.where(iota((16, 128), 0) == 4 * half + col // 8, total, 0.0), axis=0, keepdims=True
    )
    q_ref[...] = pltpu.roll(line, (128 - 16 * (col % 8)) % 128, 1)[:, :16]
    kv_ref[...] = pltpu.roll(total[8:16], (128 - 64 * half - 2 * col) % 128, 1)[:2, :2]


def unpack_kernel(back_ref, place_ref, gq_ref, gk_ref, gv_ref, q_s, k_s, v_s):
    place_row = place_ref[...].astype(F32)
    place_col = row_to_column(place_row, TOK)
    rank = jnp.sum(jnp.where(place_row < place_col, 1.0, 0.0), axis=1, keepdims=True)
    pick = jnp.where(iota((TOK, TOK), 1).astype(F32) == rank, 1.0, 0.0).astype(BF16)
    for j in range(KV_HEADS):
        head = slice(HEAD_DIM * j, HEAD_DIM * (j + 1))
        for s in range(8):
            rows = slice(16 * s, 16 * s + 16)
            q_s[rows, :] = back_ref[4 * s + j, :, 0:PART]
            total = None
            for t in range(3):
                base = PART + 256 * t
                term = back_ref[4 * ((s + 2 - t) % 8) + j, :, base : base + 256].astype(F32)
                total = term if total is None else total + term
            k_s[rows, head] = total[:, :128].astype(BF16)
            v_s[rows, head] = total[:, 128:].astype(BF16)
        gq_ref[:, PART * j : PART * (j + 1)] = dot(pick, q_s[...]).astype(BF16)
    gk_ref[...] = dot(pick, k_s[...]).astype(BF16)
    gv_ref[...] = dot(pick, v_s[...]).astype(BF16)


def any_spec():
    return pl.BlockSpec(memory_space=pltpu.HBM)


def vmem_spec():
    return pl.BlockSpec(memory_space=pltpu.VMEM)


def shape(dims, dtype):
    return jax.ShapeDtypeStruct(dims, dtype)


def swap(values, axis, step, size):
    return lax.ppermute(values, axis, [(c, c ^ step) for c in range(size)])


def rotation_tables():
    offset = jnp.arange(-TOK, 1024 + TOK, dtype=jnp.int32).astype(F32)
    powers = jnp.arange(HEAD_DIM // 2, dtype=F32) * (2.0 / HEAD_DIM)
    rates = ROPE_BASE ** (-powers)
    angle = offset[:, None] * rates[None, :]
    cosine = jnp.cos(angle)
    sine = jnp.sin(angle)
    return (
        jnp.concatenate([cosine, cosine], axis=1),
        jnp.concatenate([-sine, sine], axis=1),
    )


def attend(col_arr, recv, ups, q_bias, k_bias, v_bias):
    cos_table, sin_table = rotation_tables()
    return pl.pallas_call(
        attend_kernel,
        out_shape=[shape((TOK, PART), BF16)] * 4
        + [shape((SLAB, BACK), BF16), shape((16, HEAD_DIM), F32)],
        in_specs=[pl.BlockSpec(memory_space=pltpu.SMEM), pl.BlockSpec(memory_space=pl.ANY)] + [any_spec()] * 9,
        out_specs=[any_spec()] * 5 + [vmem_spec()],
        scratch_shapes=[
            pltpu.VMEM((SLAB, SENT), BF16),
            pltpu.VMEM((1280, HEAD_DIM), F32),
            pltpu.VMEM((1280, HEAD_DIM), F32),
            pltpu.VMEM((1, PART), F32),
            pltpu.VMEM((1, HEAD_DIM), F32),
            pltpu.VMEM((1, HEAD_DIM), F32),
            pltpu.VMEM((SLAB, PART), BF16),
            pltpu.VMEM((GROUP, SLAB, 2 * HEAD_DIM), BF16),
            pltpu.VMEM((3 * SLAB, 2 * HEAD_DIM), BF16),
            pltpu.VMEM((3 * SLAB, HEAD_DIM), BF16),
            pltpu.VMEM((HEAD_DIM, 3 * SLAB), BF16),
            pltpu.VMEM((HEAD_DIM, 3 * SLAB), BF16),
            pltpu.VMEM((3 * SLAB, HEAD_DIM), F32),
            pltpu.VMEM((3 * SLAB, HEAD_DIM), F32),
            pltpu.VMEM((QBLK, QBLK), F32),
            pltpu.VMEM((2, WINDOW, QBLK), F32),
            pltpu.VMEM((2, WINDOW, QBLK), F32),
            pltpu.VMEM((3 * SLAB, HEAD_DIM), F32),
            pltpu.VMEM((3 * SLAB, HEAD_DIM), F32),
            pltpu.VMEM((SLAB, PART), BF16),
            pltpu.VMEM((SLAB, PART), BF16),
            pltpu.VMEM((SLAB, BACK), BF16),
            pltpu.SemaphoreType.DMA((10,)),
        ],
        compiler_params=pltpu.CompilerParams(vmem_limit_bytes=60 * MIB),
        cost_estimate=pl.CostEstimate(flops=8 * 10**9, bytes_accessed=8 * MIB, transcendentals=5 * 10**6),
    )(col_arr, recv, *ups, q_bias, k_bias, v_bias, cos_table, sin_table)


def per_device(q_load, k_load, v_load, q_bias, k_bias, v_bias, place, segment, d_context):
    col = lax.axis_index("col")
    row = lax.axis_index("row")
    j = col % 4
    col_arr = col.reshape(1).astype(jnp.int32)
    smem = pl.BlockSpec(memory_space=pltpu.SMEM)

    packed = pl.pallas_call(
        pack_kernel,
        out_shape=shape((8, KV_HEADS, 16, SENT), BF16),
        in_specs=[any_spec()] * 5,
        out_specs=any_spec(),
        scratch_shapes=[
            pltpu.VMEM((TOK, Q_WIDTH), BF16),
            pltpu.VMEM((TOK, KV_WIDTH), BF16),
            pltpu.VMEM((TOK, KV_WIDTH), BF16),
            pltpu.VMEM((1, TOK), jnp.int32),
            pltpu.VMEM((1, TOK), jnp.int32),
            pltpu.VMEM((8, KV_HEADS, 16, SENT), BF16),
            pltpu.SemaphoreType.DMA((12,)),
        ],
        compiler_params=pltpu.CompilerParams(vmem_limit_bytes=60 * MIB),
        cost_estimate=pl.CostEstimate(flops=2 * 128 * 128 * 5120, bytes_accessed=5 * MIB, transcendentals=0),
    )(q_load[0], k_load[0], v_load[0], place, segment)
    recv = lax.all_to_all(
        packed.reshape(32, 16, SENT), "col", split_axis=0, concat_axis=0, tiled=True
    )

    up_own = d_context[0]
    ups = []
    for s in range(4):
        piece = lax.dynamic_slice_in_dim(up_own, PART * (j ^ s), PART, 1)
        ups.append(piece if s == 0 else swap(piece, "col", s, 32))
    attended = attend(
        col_arr, recv.reshape(SLAB, SENT), ups,
        q_bias.reshape(1, Q_WIDTH), k_bias.reshape(1, KV_WIDTH), v_bias.reshape(1, KV_WIDTH),
    )
    ctx_parts, back, bias = attended[:4], attended[4], attended[5]
    returned = lax.all_to_all(
        back.reshape(32, 16, BACK), "col", split_axis=0, concat_axis=0, tiled=True
    )
    ctx_in = [ctx_parts[0], swap(ctx_parts[1], "col", 1, 32)]
    ctx_in += [swap(ctx_parts[2], "col", 2, 32), swap(ctx_parts[3], "col", 3, 32)]
    for step in (2, 4):
        bias = bias + swap(bias, "row", step, 8)
    bias, ctx_in[2], ctx_in[3] = lax.optimization_barrier((bias, ctx_in[2], ctx_in[3]))
    context = pl.pallas_call(
        join_kernel,
        out_shape=shape((TOK, Q_WIDTH), BF16),
        in_specs=[smem] + [vmem_spec()] * 4,
        out_specs=vmem_spec(),
        compiler_params=pltpu.CompilerParams(vmem_limit_bytes=16 * MIB),
        cost_estimate=pl.CostEstimate(flops=0, bytes_accessed=2 * MIB, transcendentals=0),
    )(col_arr, *ctx_in)
    bias = bias + swap(bias, "row", 1, 8)
    bias, context = lax.optimization_barrier((bias, context))
    bias = jnp.where(j == row // 2, bias, 0.0)
    for step in (1, 2):
        bias = bias + swap(bias, "col", step, 32)
    bias = bias + (swap(bias, "col", 8, 32) + swap(bias, "col", 16, 32) + swap(bias, "col", 24, 32))
    other = swap(bias, "col", 4, 32)
    grad_q, grad_k, grad_v = pl.pallas_call(
        unpack_kernel,
        out_shape=[shape((TOK, Q_WIDTH), BF16), shape((TOK, KV_WIDTH), BF16), shape((TOK, KV_WIDTH), BF16)],
        in_specs=[vmem_spec()] * 2,
        out_specs=[vmem_spec()] * 3,
        scratch_shapes=[
            pltpu.VMEM((TOK, PART), BF16),
            pltpu.VMEM((TOK, KV_WIDTH), BF16),
            pltpu.VMEM((TOK, KV_WIDTH), BF16),
        ],
        compiler_params=pltpu.CompilerParams(vmem_limit_bytes=24 * MIB),
        cost_estimate=pl.CostEstimate(flops=2 * 128 * 128 * 5120, bytes_accessed=4 * MIB, transcendentals=0),
    )(returned, place)
    other, grad_v = lax.optimization_barrier((other, grad_v))
    bias_q, bias_kv = pl.pallas_call(
        finish_kernel,
        out_shape=[shape((1, 16), F32), shape((2, 2), F32)],
        in_specs=[smem, vmem_spec(), vmem_spec()],
        out_specs=[vmem_spec()] * 2,
        compiler_params=pltpu.CompilerParams(vmem_limit_bytes=8 * MIB),
        cost_estimate=pl.CostEstimate(flops=0, bytes_accessed=32768, transcendentals=0),
    )(jnp.stack([col, row]).astype(jnp.int32), bias, other)
    bias_q = bias_q.reshape(16)
    return (context[None], grad_q[None], grad_k[None], grad_v[None], bias_q, bias_kv)


def solution(mesh):
    return jax.shard_map(
        per_device,
        mesh=mesh,
        in_specs=(
            P("row", "col", None),
            P("row", "col", None),
            P("row", "col", None),
            P(),
            P(),
            P(),
            P("row", "col"),
            P("row", "col"),
            P("row", "col", None),
        ),
        out_specs=(
            P("row", "col", None),
            P("row", "col", None),
            P("row", "col", None),
            P("row", "col", None),
            P(("row", "col")),
            P(None, ("row", "col")),
        ),
        check_vma=False,
    )
```

```python
import functools

import jax
import jax.numpy as jnp
from jax import lax
from jax.experimental import pallas as pl
from jax.experimental.pallas import tpu as pltpu
from jax.sharding import PartitionSpec as P

HEADS = 32
KV_HEADS = 4
GROUP = 8
HEAD_DIM = 128
SEGS = 8
TOK = 128
SLAB = 512
QBLK = 256
KTILE = 256
WINDOW = 1280
Q_WIDTH = HEADS * HEAD_DIM
KV_WIDTH = KV_HEADS * HEAD_DIM
PART = GROUP * HEAD_DIM
SENT = PART + 6 * HEAD_DIM + 128
BACK = PART + 6 * HEAD_DIM
MIB = 1024 * 1024

ROPE_BASE = 1000000.0
MASKED = -1e30
LOG2E = 1.4426950408889634
F32 = jnp.float32
BF16 = jnp.bfloat16

NN = (((1,), (0,)), ((), ()))
NT = (((1,), (1,)), ((), ()))


def dot(a, b, dims=NN):
    return lax.dot_general(a, b, dims, preferred_element_type=F32)


def iota(shape, axis):
    return lax.broadcasted_iota(jnp.int32, shape, axis)


def row_to_column(row, size):
    same = iota((size, size), 0) == iota((size, size), 1)
    return jnp.sum(jnp.where(same, row, 0.0), axis=1, keepdims=True)


def pack_kernel(q_hbm, k_hbm, v_hbm, place_hbm, seg_hbm, out_hbm, q_s, k_s, v_s, place_s, seg_s, out_s, sems):
    names = [(place_hbm, place_s), (seg_hbm, seg_s), (k_hbm, k_s), (v_hbm, v_s)]
    loads = [pltpu.make_async_copy(src, dst, sems.at[n]) for n, (src, dst) in enumerate(names)]
    for j in range(KV_HEADS):
        lanes = slice(PART * j, PART * (j + 1))
        loads.append(pltpu.make_async_copy(q_hbm.at[:, lanes], q_s.at[:, lanes], sems.at[4 + j]))
    for load in loads:
        load.start()
    loads[0].wait()
    loads[1].wait()
    place_row = place_s[...].astype(F32)
    place_col = row_to_column(place_row, TOK)
    rank = jnp.sum(jnp.where(place_col < place_row, 1.0, 0.0), axis=0, keepdims=True)
    pick = iota((TOK, TOK), 0).astype(F32) == rank
    pick_low = jnp.where(pick, 1.0, 0.0).astype(BF16)
    ranked = jnp.sum(jnp.where(pick, place_row, 0.0), axis=1, keepdims=True)
    inside = ranked - ((iota((TOK, 1), 0) // 16) * SLAB).astype(F32)
    high = jnp.floor(inside * (1.0 / 128.0))
    low = inside - 128.0 * high
    seg_col = row_to_column(seg_s[...].astype(F32), TOK)
    lane = iota((TOK, 128), 1)
    below = jnp.sum(
        jnp.where(seg_col < (lane - 8).astype(F32), 1.0, 0.0), axis=0, keepdims=True
    )
    lane16 = iota((16, 128), 1)
    counts = jnp.where(iota((16, 128), 0) == 0, below, 0.0)
    metas = []
    for z in range(8):
        meta = counts
        for t in range(3):
            s = (z - 2 + t) % 8
            rows = slice(16 * s, 16 * s + 16)
            meta = jnp.where(lane16 == 2 * t, high[rows], meta)
            meta = jnp.where(lane16 == 2 * t + 1, low[rows], meta)
        metas.append(meta.astype(BF16))
    loads[2].wait()
    loads[3].wait()
    keys = dot(pick_low, k_s[...]).astype(BF16)
    vals = dot(pick_low, v_s[...]).astype(BF16)
    stores = []
    for j in range(KV_HEADS):
        loads[4 + j].wait()
        part = dot(pick_low, q_s[:, PART * j : PART * (j + 1)]).astype(BF16)
        head = slice(HEAD_DIM * j, HEAD_DIM * (j + 1))
        for z in range(8):
            out_s[z, j, :, 0:PART] = part[16 * z : 16 * z + 16]
            for t in range(3):
                s = (z - 2 + t) % 8
                rows = slice(16 * s, 16 * s + 16)
                base = PART + 256 * t
                out_s[z, j, :, base : base + 128] = keys[rows, head]
                out_s[z, j, :, base + 128 : base + 256] = vals[rows, head]
            out_s[z, j, :, BACK:SENT] = metas[z]
        store = pltpu.make_async_copy(out_s.at[:, j], out_hbm.at[:, j], sems.at[8 + j])
        store.start()
        stores.append(store)
    for store in stores:
        store.wait()


def turn(values, cosine, sine):
    return values * cosine + pltpu.roll(values, HEAD_DIM // 2, 1) * sine


def unturn(values, cosine, sine):
    return values * cosine - pltpu.roll(values, HEAD_DIM // 2, 1) * sine


def attend_kernel(
    col_ref, recv_hbm, up0, up1, up2, up3, qb_hbm, kb_hbm, vb_hbm, cos_hbm, sin_hbm,
    ctx0, ctx1, ctx2, ctx3, back_hbm, bias_ref,
    recv_s, cos_t, sin_t, qb_s, kb_s, vb_s,
    up_s, q_s, k_s, v_s, kt_s, vt_s, cos_s, sin_s, mask_s, s_s, p_s, dk_s, dv_s, ctx_s, dq_s, back_s, sems,
):
    col = col_ref[0]
    z = col // 4
    j = col % 4
    first = SLAB * (z - 2)
    scale = HEAD_DIM ** (-0.5)

    copies = [
        pltpu.make_async_copy(recv_hbm, recv_s, sems.at[0]),
        pltpu.make_async_copy(cos_hbm, cos_t, sems.at[1]),
        pltpu.make_async_copy(sin_hbm, sin_t, sems.at[2]),
        pltpu.make_async_copy(kb_hbm.at[:, pl.ds(pl.multiple_of(HEAD_DIM * j, HEAD_DIM), HEAD_DIM)], kb_s, sems.at[3]),
        pltpu.make_async_copy(vb_hbm.at[:, pl.ds(pl.multiple_of(HEAD_DIM * j, HEAD_DIM), HEAD_DIM)], vb_s, sems.at[4]),
        pltpu.make_async_copy(qb_hbm.at[:, pl.ds(pl.multiple_of(PART * j, PART), PART)], qb_s, sems.at[5]),
    ]
    for s, ref in enumerate((up0, up1, up2, up3)):
        copies.append(
            pltpu.make_async_copy(
                ref, up_s.at[pl.ds(pl.multiple_of(TOK * (j ^ s), TOK), TOK), :], sems.at[6 + s]
            )
        )
    for copy in copies:
        copy.start()
    dk_s[...] = jnp.zeros_like(dk_s)
    dv_s[...] = jnp.zeros_like(dv_s)
    cos_s[...] = jnp.zeros_like(cos_s)
    sin_s[...] = jnp.zeros_like(sin_s)
    mask_s[...] = jnp.where(iota((QBLK, QBLK), 0) <= iota((QBLK, QBLK), 1), 0.0, MASKED)
    for copy in copies[:6]:
        copy.wait()

    meta = recv_s[:, BACK:SENT].astype(F32)
    meta_rows = jnp.transpose(meta)
    sums = jnp.sum(meta, axis=0, keepdims=True)
    starts = [jnp.sum(meta[:, 8 + v : 9 + v]).astype(jnp.int32) for v in range(SEGS)]

    for b in range(12):
        at = first + TOK * b
        rows = slice(TOK * b, TOK * (b + 1))
        for v in range(SEGS):
            begin = starts[v]
            end = starts[v + 1] if v + 1 < SEGS else jnp.int32(8 * SLAB)

            @pl.when((begin < at + TOK) & (end > at))
            def _():
                src = pl.ds(at - begin + TOK, TOK)
                inside = at + iota((TOK, HEAD_DIM), 0) >= begin
                cos_s[rows, :] = jnp.where(inside, cos_t[src, :], cos_s[rows, :])
                sin_s[rows, :] = jnp.where(inside, sin_t[src, :], sin_s[rows, :])

    lane = iota((1, HEAD_DIM), 1)
    named = (lane >= 8) & (lane < 16)
    lower = jnp.where(named, sums, 1e9)
    upper = jnp.where(named, jnp.where(lane == 15, 8.0 * SLAB, pltpu.roll(sums, HEAD_DIM - 1, 1)), -1e9)
    upper = jnp.where(lane == 16, 0.0, upper)
    lower = jnp.where(lane == 16, -1e9, lower)
    spot = iota((SLAB, SLAB), 0).astype(F32)
    for t in range(3):
        pos = meta_rows[2 * t : 2 * t + 1] * 128.0 + meta_rows[2 * t + 1 : 2 * t + 2]
        pick = jnp.where(spot == pos, 1.0, 0.0).astype(BF16)
        rows = slice(SLAB * t, SLAB * (t + 1))
        base = PART + 256 * t
        both = dot(pick, recv_s[:, base : base + 256])
        keys = turn(both[:, :128] + kb_s[...], cos_s[rows, :], sin_s[rows, :])
        vals = both[:, 128:] + vb_s[...]
        at = (first + SLAB * t + iota((SLAB, HEAD_DIM), 0)).astype(F32)
        name = jnp.where((at >= lower) & (at < upper), 1.0, 0.0)
        k_s[rows, 0:HEAD_DIM] = keys.astype(BF16)
        k_s[rows, HEAD_DIM:] = name.astype(BF16)
        v_s[rows, :] = vals.astype(BF16)
        kt_s[:, rows] = jnp.transpose(keys).astype(BF16)
        vt_s[:, rows] = jnp.transpose(vals).astype(BF16)
        if t == 2:
            other = jnp.where((lane >= 8) & (lane < 17), MASKED * (1.0 - name), 0.0).astype(BF16)
            for pair in range(4):
                lanes = slice(256 * pair, 256 * (pair + 1))
                both = dot(pick, recv_s[:, lanes]) + qb_s[:, lanes]
                for u in range(2):
                    one = both[:, 128 * u : 128 * (u + 1)]
                    q_s[2 * pair + u, :, 0:HEAD_DIM] = turn(one, cos_s[rows, :], sin_s[rows, :]).astype(BF16)
                    q_s[2 * pair + u, :, HEAD_DIM:] = other

    for copy in copies[6:]:
        copy.wait()

    def one_head(h, spans):
        lanes = pl.ds(pl.multiple_of(h * HEAD_DIM, HEAD_DIM), HEAD_DIM)
        blocks = range(2)
        q_rows = [slice(QBLK * i, QBLK * (i + 1)) for i in blocks]
        k_rows = [slice(begin, begin + size) for begin, size in spans]
        size = [span[1] for span in spans]
        query = [q_s[h, q_rows[i], 0:HEAD_DIM] for i in blocks]
        up = [up_s[q_rows[i], lanes] for i in blocks]
        up_t = [jnp.transpose(up[i].astype(F32)) for i in blocks]
        top = [None, None]
        invert = [None, None]
        out_low = [None, None]
        dq_t = [None, None]
        for i in blocks:
            edge = size[i] - QBLK
            score = dot(k_s[k_rows[i], :], q_s[h, q_rows[i], :], NT)
            s_s[i, 0:edge, :] = score[:edge]
            last = score[edge:] + mask_s[...]
            s_s[i, edge : size[i], :] = last
            top[i] = jnp.maximum(
                jnp.max(score[:edge], axis=0, keepdims=True), jnp.max(last, axis=0, keepdims=True)
            )
        for i in blocks:
            p_s[i, 0 : size[i], :] = dot(v_s[k_rows[i], :], up[i], NT)
        for i in blocks:
            weight = jnp.exp2((s_s[i, 0 : size[i], :] - top[i]) * (scale * LOG2E))
            s_s[i, 0 : size[i], :] = weight
            invert[i] = 1.0 / jnp.sum(weight, axis=0, keepdims=True)
        for i in blocks:
            prob_low = (s_s[i, 0 : size[i], :] * invert[i]).astype(BF16)
            out_t = dot(vt_s[:, k_rows[i]], prob_low)
            dv_s[k_rows[i], :] += dot(prob_low, up[i])
            out_low[i] = out_t.astype(BF16).astype(F32)
        for i in blocks:
            ctx_s[q_rows[i], lanes] = jnp.transpose(out_low[i]).astype(BF16)
            delta = jnp.sum(up_t[i] * out_low[i], axis=0, keepdims=True)
            prob = s_s[i, 0 : size[i], :] * invert[i]
            dscore = (prob * (p_s[i, 0 : size[i], :] - delta)).astype(BF16)
            dq_t[i] = dot(kt_s[:, k_rows[i]], dscore)
            dk_s[k_rows[i], :] += dot(dscore, query[i])
        total = None
        for i in blocks:
            dq = jnp.transpose(dq_t[i]) * scale
            w_rows = slice(2 * SLAB + QBLK * i, 2 * SLAB + QBLK * (i + 1))
            dq = unturn(dq, cos_s[w_rows, :], sin_s[w_rows, :])
            dq_s[q_rows[i], lanes] = dq.astype(BF16)
            mine = jnp.sum(dq, axis=0, keepdims=True)
            total = mine if total is None else total + mine
        bias_ref[pl.ds(h, 1), :] = total

    def all_heads(spans):
        def step(h, _):
            one_head(h, spans)
            return 0

        lax.fori_loop(0, GROUP, step, 0, unroll=2)

    middle = SLAB * z + QBLK
    begin = jnp.int32(0)
    for v in range(1, SEGS):
        begin = jnp.where(starts[v] <= middle, starts[v], begin)
    far = begin < middle - (WINDOW - 2 * QBLK)

    @pl.when(far)
    def _():
        all_heads(((QBLK, WINDOW - QBLK), (QBLK, WINDOW)))

    @pl.when(jnp.logical_not(far))
    def _():
        all_heads(((0, WINDOW), (2 * QBLK, WINDOW - QBLK)))

    outs = []
    for s, ref in enumerate((ctx0, ctx1, ctx2, ctx3)):
        outs.append(
            pltpu.make_async_copy(
                ctx_s.at[pl.ds(pl.multiple_of(TOK * (j ^ s), TOK), TOK), :], ref, sems.at[6 + s]
            )
        )
    for copy in outs:
        copy.start()

    sum_k = jnp.zeros((1, HEAD_DIM), F32)
    sum_v = jnp.zeros((1, HEAD_DIM), F32)
    across = iota((SLAB, SLAB), 1).astype(F32)
    for t in (2, 0, 1):
        rows = slice(SLAB * t, SLAB * (t + 1))
        pos = meta[:, 2 * t : 2 * t + 1] * 128.0 + meta[:, 2 * t + 1 : 2 * t + 2]
        drop = jnp.where(across == pos, 1.0, 0.0).astype(BF16)
        if t == 2:
            back_s[:, 0:PART] = dot(drop, dq_s[...]).astype(BF16)
            main = pltpu.make_async_copy(back_s.at[:, 0:PART], back_hbm.at[:, 0:PART], sems.at[0])
            main.start()
            outs.append(main)
        dk = unturn(dk_s[rows, :] * scale, cos_s[rows, :], sin_s[rows, :])
        dv = dv_s[rows, :]
        sum_k = sum_k + jnp.sum(dk, axis=0, keepdims=True)
        sum_v = sum_v + jnp.sum(dv, axis=0, keepdims=True)
        base = PART + 256 * t
        both = jnp.concatenate([dk.astype(BF16), dv.astype(BF16)], axis=1)
        back_s[:, base : base + 256] = dot(drop, both).astype(BF16)
        side = pltpu.make_async_copy(back_s.at[:, base : base + 256], back_hbm.at[:, base : base + 256], sems.at[1 + t])
        side.start()
        outs.append(side)
    bias_ref[8:9, :] = sum_k
    bias_ref[9:10, :] = sum_v
    bias_ref[10:16, :] = jnp.zeros((6, HEAD_DIM), F32)
    for copy in outs:
        copy.wait()


def join_kernel(col_ref, c0, c1, c2, c3, out_ref):
    j = col_ref[0] % 4
    for s, ref in enumerate((c0, c1, c2, c3)):
        out_ref[:, pl.ds(pl.multiple_of(PART * (j ^ s), PART), PART)] = ref[...]


def finish_kernel(at_ref, mine_ref, other_ref, q_ref, kv_ref):
    col = at_ref[0]
    half = at_ref[1] % 2
    total = mine_ref[...] + other_ref[...]
    line = jnp.sum(
        jnp.where(iota((16, 128), 0) == 4 * half + col // 8, total, 0.0), axis=0, keepdims=True
    )
    q_ref[...] = pltpu.roll(line, (128 - 16 * (col % 8)) % 128, 1)[:, :16]
    kv_ref[...] = pltpu.roll(total[8:16], (128 - 64 * half - 2 * col) % 128, 1)[:2, :2]


def unpack_kernel(back_ref, place_ref, gq_ref, gk_ref, gv_ref, q_s, k_s, v_s):
    place_row = place_ref[...].astype(F32)
    place_col = row_to_column(place_row, TOK)
    rank = jnp.sum(jnp.where(place_row < place_col, 1.0, 0.0), axis=1, keepdims=True)
    pick = jnp.where(iota((TOK, TOK), 1).astype(F32) == rank, 1.0, 0.0).astype(BF16)
    for j in range(KV_HEADS):
        head = slice(HEAD_DIM * j, HEAD_DIM * (j + 1))
        for s in range(8):
            rows = slice(16 * s, 16 * s + 16)
            q_s[rows, :] = back_ref[4 * s + j, :, 0:PART]
            total = None
            for t in range(3):
                base = PART + 256 * t
                term = back_ref[4 * ((s + 2 - t) % 8) + j, :, base : base + 256].astype(F32)
                total = term if total is None else total + term
            k_s[rows, head] = total[:, :128].astype(BF16)
            v_s[rows, head] = total[:, 128:].astype(BF16)
        gq_ref[:, PART * j : PART * (j + 1)] = dot(pick, q_s[...]).astype(BF16)
    gk_ref[...] = dot(pick, k_s[...]).astype(BF16)
    gv_ref[...] = dot(pick, v_s[...]).astype(BF16)


def any_spec():
    return pl.BlockSpec(memory_space=pltpu.HBM)


def vmem_spec():
    return pl.BlockSpec(memory_space=pltpu.VMEM)


def shape(dims, dtype):
    return jax.ShapeDtypeStruct(dims, dtype)


def swap(values, axis, step, size):
    return lax.ppermute(values, axis, [(c, c ^ step) for c in range(size)])


def rotation_tables():
    offset = jnp.arange(-TOK, 1024 + TOK, dtype=jnp.int32).astype(F32)
    powers = jnp.arange(HEAD_DIM // 2, dtype=F32) * (2.0 / HEAD_DIM)
    rates = ROPE_BASE ** (-powers)
    angle = offset[:, None] * rates[None, :]
    cosine = jnp.cos(angle)
    sine = jnp.sin(angle)
    return (
        jnp.concatenate([cosine, cosine], axis=1),
        jnp.concatenate([-sine, sine], axis=1),
    )


def attend(col_arr, recv, ups, q_bias, k_bias, v_bias):
    cos_table, sin_table = rotation_tables()
    return pl.pallas_call(
        attend_kernel,
        out_shape=[shape((TOK, PART), BF16)] * 4
        + [shape((SLAB, BACK), BF16), shape((16, HEAD_DIM), F32)],
        in_specs=[pl.BlockSpec(memory_space=pltpu.SMEM), pl.BlockSpec(memory_space=pl.ANY)] + [any_spec()] * 9,
        out_specs=[any_spec()] * 5 + [vmem_spec()],
        scratch_shapes=[
            pltpu.VMEM((SLAB, SENT), BF16),
            pltpu.VMEM((1280, HEAD_DIM), F32),
            pltpu.VMEM((1280, HEAD_DIM), F32),
            pltpu.VMEM((1, PART), F32),
            pltpu.VMEM((1, HEAD_DIM), F32),
            pltpu.VMEM((1, HEAD_DIM), F32),
            pltpu.VMEM((SLAB, PART), BF16),
            pltpu.VMEM((GROUP, SLAB, 2 * HEAD_DIM), BF16),
            pltpu.VMEM((3 * SLAB, 2 * HEAD_DIM), BF16),
            pltpu.VMEM((3 * SLAB, HEAD_DIM), BF16),
            pltpu.VMEM((HEAD_DIM, 3 * SLAB), BF16),
            pltpu.VMEM((HEAD_DIM, 3 * SLAB), BF16),
            pltpu.VMEM((3 * SLAB, HEAD_DIM), F32),
            pltpu.VMEM((3 * SLAB, HEAD_DIM), F32),
            pltpu.VMEM((QBLK, QBLK), F32),
            pltpu.VMEM((2, WINDOW, QBLK), F32),
            pltpu.VMEM((2, WINDOW, QBLK), F32),
            pltpu.VMEM((3 * SLAB, HEAD_DIM), F32),
            pltpu.VMEM((3 * SLAB, HEAD_DIM), F32),
            pltpu.VMEM((SLAB, PART), BF16),
            pltpu.VMEM((SLAB, PART), BF16),
            pltpu.VMEM((SLAB, BACK), BF16),
            pltpu.SemaphoreType.DMA((10,)),
        ],
        compiler_params=pltpu.CompilerParams(vmem_limit_bytes=50 * MIB),
        cost_estimate=pl.CostEstimate(flops=8 * 10**9, bytes_accessed=8 * MIB, transcendentals=5 * 10**6),
    )(col_arr, recv, *ups, q_bias, k_bias, v_bias, cos_table, sin_table)


def per_device(q_load, k_load, v_load, q_bias, k_bias, v_bias, place, segment, d_context):
    col = lax.axis_index("col")
    row = lax.axis_index("row")
    j = col % 4
    col_arr = col.reshape(1).astype(jnp.int32)
    smem = pl.BlockSpec(memory_space=pltpu.SMEM)

    packed = pl.pallas_call(
        pack_kernel,
        out_shape=shape((8, KV_HEADS, 16, SENT), BF16),
        in_specs=[any_spec()] * 5,
        out_specs=any_spec(),
        scratch_shapes=[
            pltpu.VMEM((TOK, Q_WIDTH), BF16),
            pltpu.VMEM((TOK, KV_WIDTH), BF16),
            pltpu.VMEM((TOK, KV_WIDTH), BF16),
            pltpu.VMEM((1, TOK), jnp.int32),
            pltpu.VMEM((1, TOK), jnp.int32),
            pltpu.VMEM((8, KV_HEADS, 16, SENT), BF16),
            pltpu.SemaphoreType.DMA((12,)),
        ],
        compiler_params=pltpu.CompilerParams(vmem_limit_bytes=60 * MIB),
        cost_estimate=pl.CostEstimate(flops=2 * 128 * 128 * 5120, bytes_accessed=5 * MIB, transcendentals=0),
    )(q_load[0], k_load[0], v_load[0], place, segment)
    recv = lax.all_to_all(
        packed.reshape(32, 16, SENT), "col", split_axis=0, concat_axis=0, tiled=True
    )

    up_own = d_context[0]
    ups = []
    for s in range(4):
        piece = lax.dynamic_slice_in_dim(up_own, PART * (j ^ s), PART, 1)
        ups.append(piece if s == 0 else swap(piece, "col", s, 32))
    attended = attend(
        col_arr, recv.reshape(SLAB, SENT), ups,
        q_bias.reshape(1, Q_WIDTH), k_bias.reshape(1, KV_WIDTH), v_bias.reshape(1, KV_WIDTH),
    )
    ctx_parts, back, bias = attended[:4], attended[4], attended[5]
    returned = lax.all_to_all(
        back.reshape(32, 16, BACK), "col", split_axis=0, concat_axis=0, tiled=True
    )
    ctx_in = [ctx_parts[0], swap(ctx_parts[1], "col", 1, 32)]
    ctx_in += [swap(ctx_parts[2], "col", 2, 32), swap(ctx_parts[3], "col", 3, 32)]
    for step in (2, 4):
        bias = bias + swap(bias, "row", step, 8)
    bias, ctx_in[2], ctx_in[3] = lax.optimization_barrier((bias, ctx_in[2], ctx_in[3]))
    context = pl.pallas_call(
        join_kernel,
        out_shape=shape((TOK, Q_WIDTH), BF16),
        in_specs=[smem] + [vmem_spec()] * 4,
        out_specs=vmem_spec(),
        compiler_params=pltpu.CompilerParams(vmem_limit_bytes=16 * MIB),
        cost_estimate=pl.CostEstimate(flops=0, bytes_accessed=2 * MIB, transcendentals=0),
    )(col_arr, *ctx_in)
    bias = bias + swap(bias, "row", 1, 8)
    bias, context = lax.optimization_barrier((bias, context))
    bias = jnp.where(j == row // 2, bias, 0.0)
    for step in (1, 2):
        bias = bias + swap(bias, "col", step, 32)
    bias = bias + (swap(bias, "col", 8, 32) + swap(bias, "col", 16, 32) + swap(bias, "col", 24, 32))
    other = swap(bias, "col", 4, 32)
    grad_q, grad_k, grad_v = pl.pallas_call(
        unpack_kernel,
        out_shape=[shape((TOK, Q_WIDTH), BF16), shape((TOK, KV_WIDTH), BF16), shape((TOK, KV_WIDTH), BF16)],
        in_specs=[vmem_spec()] * 2,
        out_specs=[vmem_spec()] * 3,
        scratch_shapes=[
            pltpu.VMEM((TOK, PART), BF16),
            pltpu.VMEM((TOK, KV_WIDTH), BF16),
            pltpu.VMEM((TOK, KV_WIDTH), BF16),
        ],
        compiler_params=pltpu.CompilerParams(vmem_limit_bytes=24 * MIB),
        cost_estimate=pl.CostEstimate(flops=2 * 128 * 128 * 5120, bytes_accessed=4 * MIB, transcendentals=0),
    )(returned, place)
    other, grad_v = lax.optimization_barrier((other, grad_v))
    bias_q, bias_kv = pl.pallas_call(
        finish_kernel,
        out_shape=[shape((1, 16), F32), shape((2, 2), F32)],
        in_specs=[smem, vmem_spec(), vmem_spec()],
        out_specs=[vmem_spec()] * 2,
        compiler_params=pltpu.CompilerParams(vmem_limit_bytes=8 * MIB),
        cost_estimate=pl.CostEstimate(flops=0, bytes_accessed=32768, transcendentals=0),
    )(jnp.stack([col, row]).astype(jnp.int32), bias, other)
    bias_q = bias_q.reshape(16)
    return (context[None], grad_q[None], grad_k[None], grad_v[None], bias_q, bias_kv)


def solution(mesh):
    return jax.shard_map(
        per_device,
        mesh=mesh,
        in_specs=(
            P("row", "col", None),
            P("row", "col", None),
            P("row", "col", None),
            P(),
            P(),
            P(),
            P("row", "col"),
            P("row", "col"),
            P("row", "col", None),
        ),
        out_specs=(
            P("row", "col", None),
            P("row", "col", None),
            P("row", "col", None),
            P("row", "col", None),
            P(("row", "col")),
            P(None, ("row", "col")),
        ),
        check_vma=False,
    )
```

```python
import functools

import jax
import jax.numpy as jnp
from jax import lax
from jax.experimental import pallas as pl
from jax.experimental.pallas import tpu as pltpu
from jax.sharding import PartitionSpec as P

HEADS = 32
KV_HEADS = 4
GROUP = 8
HEAD_DIM = 128
SEGS = 8
TOK = 128
SLAB = 512
QBLK = 256
KTILE = 256
WINDOW = 1280
Q_WIDTH = HEADS * HEAD_DIM
KV_WIDTH = KV_HEADS * HEAD_DIM
PART = GROUP * HEAD_DIM
SENT = PART + 6 * HEAD_DIM + 128
BACK = PART + 6 * HEAD_DIM
MIB = 1024 * 1024

ROPE_BASE = 1000000.0
MASKED = -1e30
LOG2E = 1.4426950408889634
F32 = jnp.float32
BF16 = jnp.bfloat16

NN = (((1,), (0,)), ((), ()))
NT = (((1,), (1,)), ((), ()))


def dot(a, b, dims=NN):
    return lax.dot_general(a, b, dims, preferred_element_type=F32)


def iota(shape, axis):
    return lax.broadcasted_iota(jnp.int32, shape, axis)


def row_to_column(row, size):
    same = iota((size, size), 0) == iota((size, size), 1)
    return jnp.sum(jnp.where(same, row, 0.0), axis=1, keepdims=True)


def pack_kernel(q_hbm, k_hbm, v_hbm, place_hbm, seg_hbm, out_hbm, q_s, k_s, v_s, place_s, seg_s, out_s, sems):
    names = [(place_hbm, place_s), (seg_hbm, seg_s), (k_hbm, k_s), (v_hbm, v_s)]
    loads = [pltpu.make_async_copy(src, dst, sems.at[n]) for n, (src, dst) in enumerate(names)]
    for j in range(KV_HEADS):
        lanes = slice(PART * j, PART * (j + 1))
        loads.append(pltpu.make_async_copy(q_hbm.at[:, lanes], q_s.at[:, lanes], sems.at[4 + j]))
    for load in loads:
        load.start()
    loads[0].wait()
    loads[1].wait()
    place_row = place_s[...].astype(F32)
    place_col = row_to_column(place_row, TOK)
    rank = jnp.sum(jnp.where(place_col < place_row, 1.0, 0.0), axis=0, keepdims=True)
    pick = iota((TOK, TOK), 0).astype(F32) == rank
    pick_low = jnp.where(pick, 1.0, 0.0).astype(BF16)
    ranked = jnp.sum(jnp.where(pick, place_row, 0.0), axis=1, keepdims=True)
    inside = ranked - ((iota((TOK, 1), 0) // 16) * SLAB).astype(F32)
    high = jnp.floor(inside * (1.0 / 128.0))
    low = inside - 128.0 * high
    seg_col = row_to_column(seg_s[...].astype(F32), TOK)
    lane = iota((TOK, 128), 1)
    below = jnp.sum(
        jnp.where(seg_col < (lane - 8).astype(F32), 1.0, 0.0), axis=0, keepdims=True
    )
    lane16 = iota((16, 128), 1)
    counts = jnp.where(iota((16, 128), 0) == 0, below, 0.0)
    metas = []
    for z in range(8):
        meta = counts
        for t in range(3):
            s = (z - 2 + t) % 8
            rows = slice(16 * s, 16 * s + 16)
            meta = jnp.where(lane16 == 2 * t, high[rows], meta)
            meta = jnp.where(lane16 == 2 * t + 1, low[rows], meta)
        metas.append(meta.astype(BF16))
    loads[2].wait()
    loads[3].wait()
    keys = dot(pick_low, k_s[...]).astype(BF16)
    vals = dot(pick_low, v_s[...]).astype(BF16)
    stores = []
    for j in range(KV_HEADS):
        loads[4 + j].wait()
        part = dot(pick_low, q_s[:, PART * j : PART * (j + 1)]).astype(BF16)
        head = slice(HEAD_DIM * j, HEAD_DIM * (j + 1))
        for z in range(8):
            out_s[z, j, :, 0:PART] = part[16 * z : 16 * z + 16]
            for t in range(3):
                s = (z - 2 + t) % 8
                rows = slice(16 * s, 16 * s + 16)
                base = PART + 256 * t
                out_s[z, j, :, base : base + 128] = keys[rows, head]
                out_s[z, j, :, base + 128 : base + 256] = vals[rows, head]
            out_s[z, j, :, BACK:SENT] = metas[z]
        store = pltpu.make_async_copy(out_s.at[:, j], out_hbm.at[:, j], sems.at[8 + j])
        store.start()
        stores.append(store)
    for store in stores:
        store.wait()


def turn(values, cosine, sine):
    return values * cosine + pltpu.roll(values, HEAD_DIM // 2, 1) * sine


def unturn(values, cosine, sine):
    return values * cosine - pltpu.roll(values, HEAD_DIM // 2, 1) * sine


def attend_kernel(
    col_ref, recv_hbm, up0, up1, up2, up3, qb_hbm, kb_hbm, vb_hbm, cos_hbm, sin_hbm,
    ctx0, ctx1, ctx2, ctx3, back_hbm, bias_ref,
    recv_s, cos_t, sin_t, qb_s, kb_s, vb_s,
    up_s, q_s, k_s, v_s, kt_s, vt_s, cos_s, sin_s, mask_s, s_s, p_s, dk_s, dv_s, ctx_s, dq_s, back_s, sems,
):
    col = col_ref[0]
    z = col // 4
    j = col % 4
    first = SLAB * (z - 2)
    scale = HEAD_DIM ** (-0.5)

    copies = [
        pltpu.make_async_copy(recv_hbm.at[:, PART:SENT], recv_s.at[:, PART:SENT], sems.at[0]),
        pltpu.make_async_copy(cos_hbm, cos_t, sems.at[1]),
        pltpu.make_async_copy(sin_hbm, sin_t, sems.at[2]),
        pltpu.make_async_copy(kb_hbm.at[:, pl.ds(pl.multiple_of(HEAD_DIM * j, HEAD_DIM), HEAD_DIM)], kb_s, sems.at[3]),
        pltpu.make_async_copy(vb_hbm.at[:, pl.ds(pl.multiple_of(HEAD_DIM * j, HEAD_DIM), HEAD_DIM)], vb_s, sems.at[4]),
        pltpu.make_async_copy(qb_hbm.at[:, pl.ds(pl.multiple_of(PART * j, PART), PART)], qb_s, sems.at[5]),
    ]
    for s, ref in enumerate((up0, up1, up2, up3)):
        copies.append(
            pltpu.make_async_copy(
                ref, up_s.at[pl.ds(pl.multiple_of(TOK * (j ^ s), TOK), TOK), :], sems.at[6 + s]
            )
        )
    copies.append(
        pltpu.make_async_copy(recv_hbm.at[:, 0:PART], recv_s.at[:, 0:PART], sems.at[10])
    )
    for copy in copies:
        copy.start()
    dk_s[...] = jnp.zeros_like(dk_s)
    dv_s[...] = jnp.zeros_like(dv_s)
    cos_s[...] = jnp.zeros_like(cos_s)
    sin_s[...] = jnp.zeros_like(sin_s)
    mask_s[...] = jnp.where(iota((QBLK, QBLK), 0) <= iota((QBLK, QBLK), 1), 0.0, MASKED)
    for copy in copies[:6]:
        copy.wait()

    meta = recv_s[:, BACK:SENT].astype(F32)
    meta_rows = jnp.transpose(meta)
    sums = jnp.sum(meta, axis=0, keepdims=True)
    starts = [jnp.sum(meta[:, 8 + v : 9 + v]).astype(jnp.int32) for v in range(SEGS)]

    for b in range(12):
        at = first + TOK * b
        rows = slice(TOK * b, TOK * (b + 1))
        for v in range(SEGS):
            begin = starts[v]
            end = starts[v + 1] if v + 1 < SEGS else jnp.int32(8 * SLAB)

            @pl.when((begin < at + TOK) & (end > at))
            def _():
                src = pl.ds(at - begin + TOK, TOK)
                inside = at + iota((TOK, HEAD_DIM), 0) >= begin
                cos_s[rows, :] = jnp.where(inside, cos_t[src, :], cos_s[rows, :])
                sin_s[rows, :] = jnp.where(inside, sin_t[src, :], sin_s[rows, :])

    lane = iota((1, HEAD_DIM), 1)
    named = (lane >= 8) & (lane < 16)
    lower = jnp.where(named, sums, 1e9)
    upper = jnp.where(named, jnp.where(lane == 15, 8.0 * SLAB, pltpu.roll(sums, HEAD_DIM - 1, 1)), -1e9)
    upper = jnp.where(lane == 16, 0.0, upper)
    lower = jnp.where(lane == 16, -1e9, lower)
    spot = iota((SLAB, SLAB), 0).astype(F32)
    for t in range(3):
        pos = meta_rows[2 * t : 2 * t + 1] * 128.0 + meta_rows[2 * t + 1 : 2 * t + 2]
        pick = jnp.where(spot == pos, 1.0, 0.0).astype(BF16)
        rows = slice(SLAB * t, SLAB * (t + 1))
        base = PART + 256 * t
        both = dot(pick, recv_s[:, base : base + 256])
        keys = turn(both[:, :128] + kb_s[...], cos_s[rows, :], sin_s[rows, :])
        vals = both[:, 128:] + vb_s[...]
        at = (first + SLAB * t + iota((SLAB, HEAD_DIM), 0)).astype(F32)
        name = jnp.where((at >= lower) & (at < upper), 1.0, 0.0)
        k_s[rows, 0:HEAD_DIM] = keys.astype(BF16)
        k_s[rows, HEAD_DIM:] = name.astype(BF16)
        v_s[rows, :] = vals.astype(BF16)
        kt_s[:, rows] = jnp.transpose(keys).astype(BF16)
        vt_s[:, rows] = jnp.transpose(vals).astype(BF16)
        if t == 2:
            copies[10].wait()
            other = jnp.where((lane >= 8) & (lane < 17), MASKED * (1.0 - name), 0.0).astype(BF16)
            for pair in range(4):
                lanes = slice(256 * pair, 256 * (pair + 1))
                both = dot(pick, recv_s[:, lanes]) + qb_s[:, lanes]
                for u in range(2):
                    one = both[:, 128 * u : 128 * (u + 1)]
                    q_s[2 * pair + u, :, 0:HEAD_DIM] = turn(one, cos_s[rows, :], sin_s[rows, :]).astype(BF16)
                    q_s[2 * pair + u, :, HEAD_DIM:] = other

    for copy in copies[6:10]:
        copy.wait()

    def one_head(h, spans):
        lanes = pl.ds(pl.multiple_of(h * HEAD_DIM, HEAD_DIM), HEAD_DIM)
        blocks = range(2)
        q_rows = [slice(QBLK * i, QBLK * (i + 1)) for i in blocks]
        k_rows = [slice(begin, begin + size) for begin, size in spans]
        size = [span[1] for span in spans]
        query = [q_s[h, q_rows[i], 0:HEAD_DIM] for i in blocks]
        up = [up_s[q_rows[i], lanes] for i in blocks]
        up_t = [jnp.transpose(up[i].astype(F32)) for i in blocks]
        top = [None, None]
        invert = [None, None]
        out_low = [None, None]
        dq_t = [None, None]
        for i in blocks:
            edge = size[i] - QBLK
            score = dot(k_s[k_rows[i], :], q_s[h, q_rows[i], :], NT)
            s_s[i, 0:edge, :] = score[:edge]
            last = score[edge:] + mask_s[...]
            s_s[i, edge : size[i], :] = last
            top[i] = jnp.maximum(
                jnp.max(score[:edge], axis=0, keepdims=True), jnp.max(last, axis=0, keepdims=True)
            )
        for i in blocks:
            p_s[i, 0 : size[i], :] = dot(v_s[k_rows[i], :], up[i], NT)
        for i in blocks:
            weight = jnp.exp2((s_s[i, 0 : size[i], :] - top[i]) * (scale * LOG2E))
            s_s[i, 0 : size[i], :] = weight
            invert[i] = 1.0 / jnp.sum(weight, axis=0, keepdims=True)
        for i in blocks:
            prob_low = (s_s[i, 0 : size[i], :] * invert[i]).astype(BF16)
            out_t = dot(vt_s[:, k_rows[i]], prob_low)
            dv_s[k_rows[i], :] += dot(prob_low, up[i])
            out_low[i] = out_t.astype(BF16).astype(F32)
        for i in blocks:
            ctx_s[q_rows[i], lanes] = jnp.transpose(out_low[i]).astype(BF16)
            delta = jnp.sum(up_t[i] * out_low[i], axis=0, keepdims=True)
            prob = s_s[i, 0 : size[i], :] * invert[i]
            dscore = (prob * (p_s[i, 0 : size[i], :] - delta)).astype(BF16)
            dq_t[i] = dot(kt_s[:, k_rows[i]], dscore)
            dk_s[k_rows[i], :] += dot(dscore, query[i])
        total = None
        for i in blocks:
            dq = jnp.transpose(dq_t[i]) * scale
            w_rows = slice(2 * SLAB + QBLK * i, 2 * SLAB + QBLK * (i + 1))
            dq = unturn(dq, cos_s[w_rows, :], sin_s[w_rows, :])
            dq_s[q_rows[i], lanes] = dq.astype(BF16)
            mine = jnp.sum(dq, axis=0, keepdims=True)
            total = mine if total is None else total + mine
        bias_ref[pl.ds(h, 1), :] = total

    def all_heads(spans):
        def step(h, _):
            one_head(h, spans)
            return 0

        lax.fori_loop(0, GROUP, step, 0, unroll=2)

    middle = SLAB * z + QBLK
    begin = jnp.int32(0)
    for v in range(1, SEGS):
        begin = jnp.where(starts[v] <= middle, starts[v], begin)
    far = begin < middle - (WINDOW - 2 * QBLK)

    @pl.when(far)
    def _():
        all_heads(((QBLK, WINDOW - QBLK), (QBLK, WINDOW)))

    @pl.when(jnp.logical_not(far))
    def _():
        all_heads(((0, WINDOW), (2 * QBLK, WINDOW - QBLK)))

    outs = []
    for s, ref in enumerate((ctx0, ctx1, ctx2, ctx3)):
        outs.append(
            pltpu.make_async_copy(
                ctx_s.at[pl.ds(pl.multiple_of(TOK * (j ^ s), TOK), TOK), :], ref, sems.at[6 + s]
            )
        )
    for copy in outs:
        copy.start()

    sum_k = jnp.zeros((1, HEAD_DIM), F32)
    sum_v = jnp.zeros((1, HEAD_DIM), F32)
    across = iota((SLAB, SLAB), 1).astype(F32)
    for t in (2, 0, 1):
        rows = slice(SLAB * t, SLAB * (t + 1))
        pos = meta[:, 2 * t : 2 * t + 1] * 128.0 + meta[:, 2 * t + 1 : 2 * t + 2]
        drop = jnp.where(across == pos, 1.0, 0.0).astype(BF16)
        if t == 2:
            back_s[:, 0:PART] = dot(drop, dq_s[...]).astype(BF16)
            main = pltpu.make_async_copy(back_s.at[:, 0:PART], back_hbm.at[:, 0:PART], sems.at[0])
            main.start()
            outs.append(main)
        dk = unturn(dk_s[rows, :] * scale, cos_s[rows, :], sin_s[rows, :])
        dv = dv_s[rows, :]
        sum_k = sum_k + jnp.sum(dk, axis=0, keepdims=True)
        sum_v = sum_v + jnp.sum(dv, axis=0, keepdims=True)
        base = PART + 256 * t
        both = jnp.concatenate([dk.astype(BF16), dv.astype(BF16)], axis=1)
        back_s[:, base : base + 256] = dot(drop, both).astype(BF16)
        side = pltpu.make_async_copy(back_s.at[:, base : base + 256], back_hbm.at[:, base : base + 256], sems.at[1 + t])
        side.start()
        outs.append(side)
    bias_ref[8:9, :] = sum_k
    bias_ref[9:10, :] = sum_v
    bias_ref[10:16, :] = jnp.zeros((6, HEAD_DIM), F32)
    for copy in outs:
        copy.wait()


def join_kernel(col_ref, c0, c1, c2, c3, out_ref):
    j = col_ref[0] % 4
    for s, ref in enumerate((c0, c1, c2, c3)):
        out_ref[:, pl.ds(pl.multiple_of(PART * (j ^ s), PART), PART)] = ref[...]


def finish_kernel(at_ref, mine_ref, other_ref, q_ref, kv_ref):
    col = at_ref[0]
    half = at_ref[1] % 2
    total = mine_ref[...] + other_ref[...]
    line = jnp.sum(
        jnp.where(iota((16, 128), 0) == 4 * half + col // 8, total, 0.0), axis=0, keepdims=True
    )
    q_ref[...] = pltpu.roll(line, (128 - 16 * (col % 8)) % 128, 1)[:, :16]
    kv_ref[...] = pltpu.roll(total[8:16], (128 - 64 * half - 2 * col) % 128, 1)[:2, :2]


def unpack_kernel(back_ref, place_ref, gq_ref, gk_ref, gv_ref, q_s, k_s, v_s):
    place_row = place_ref[...].astype(F32)
    place_col = row_to_column(place_row, TOK)
    rank = jnp.sum(jnp.where(place_row < place_col, 1.0, 0.0), axis=1, keepdims=True)
    pick = jnp.where(iota((TOK, TOK), 1).astype(F32) == rank, 1.0, 0.0).astype(BF16)
    for j in range(KV_HEADS):
        head = slice(HEAD_DIM * j, HEAD_DIM * (j + 1))
        for s in range(8):
            rows = slice(16 * s, 16 * s + 16)
            q_s[rows, :] = back_ref[4 * s + j, :, 0:PART]
            total = None
            for t in range(3):
                base = PART + 256 * t
                term = back_ref[4 * ((s + 2 - t) % 8) + j, :, base : base + 256].astype(F32)
                total = term if total is None else total + term
            k_s[rows, head] = total[:, :128].astype(BF16)
            v_s[rows, head] = total[:, 128:].astype(BF16)
        gq_ref[:, PART * j : PART * (j + 1)] = dot(pick, q_s[...]).astype(BF16)
    gk_ref[...] = dot(pick, k_s[...]).astype(BF16)
    gv_ref[...] = dot(pick, v_s[...]).astype(BF16)


def any_spec():
    return pl.BlockSpec(memory_space=pltpu.HBM)


def vmem_spec():
    return pl.BlockSpec(memory_space=pltpu.VMEM)


def shape(dims, dtype):
    return jax.ShapeDtypeStruct(dims, dtype)


def swap(values, axis, step, size):
    return lax.ppermute(values, axis, [(c, c ^ step) for c in range(size)])


def rotation_tables():
    offset = jnp.arange(-TOK, 1024 + TOK, dtype=jnp.int32).astype(F32)
    powers = jnp.arange(HEAD_DIM // 2, dtype=F32) * (2.0 / HEAD_DIM)
    rates = ROPE_BASE ** (-powers)
    angle = offset[:, None] * rates[None, :]
    cosine = jnp.cos(angle)
    sine = jnp.sin(angle)
    return (
        jnp.concatenate([cosine, cosine], axis=1),
        jnp.concatenate([-sine, sine], axis=1),
    )


def attend(col_arr, recv, ups, q_bias, k_bias, v_bias):
    cos_table, sin_table = rotation_tables()
    return pl.pallas_call(
        attend_kernel,
        out_shape=[shape((TOK, PART), BF16)] * 4
        + [shape((SLAB, BACK), BF16), shape((16, HEAD_DIM), F32)],
        in_specs=[pl.BlockSpec(memory_space=pltpu.SMEM), pl.BlockSpec(memory_space=pl.ANY)] + [any_spec()] * 9,
        out_specs=[any_spec()] * 5 + [vmem_spec()],
        scratch_shapes=[
            pltpu.VMEM((SLAB, SENT), BF16),
            pltpu.VMEM((1280, HEAD_DIM), F32),
            pltpu.VMEM((1280, HEAD_DIM), F32),
            pltpu.VMEM((1, PART), F32),
            pltpu.VMEM((1, HEAD_DIM), F32),
            pltpu.VMEM((1, HEAD_DIM), F32),
            pltpu.VMEM((SLAB, PART), BF16),
            pltpu.VMEM((GROUP, SLAB, 2 * HEAD_DIM), BF16),
            pltpu.VMEM((3 * SLAB, 2 * HEAD_DIM), BF16),
            pltpu.VMEM((3 * SLAB, HEAD_DIM), BF16),
            pltpu.VMEM((HEAD_DIM, 3 * SLAB), BF16),
            pltpu.VMEM((HEAD_DIM, 3 * SLAB), BF16),
            pltpu.VMEM((3 * SLAB, HEAD_DIM), F32),
            pltpu.VMEM((3 * SLAB, HEAD_DIM), F32),
            pltpu.VMEM((QBLK, QBLK), F32),
            pltpu.VMEM((2, WINDOW, QBLK), F32),
            pltpu.VMEM((2, WINDOW, QBLK), F32),
            pltpu.VMEM((3 * SLAB, HEAD_DIM), F32),
            pltpu.VMEM((3 * SLAB, HEAD_DIM), F32),
            pltpu.VMEM((SLAB, PART), BF16),
            pltpu.VMEM((SLAB, PART), BF16),
            pltpu.VMEM((SLAB, BACK), BF16),
            pltpu.SemaphoreType.DMA((11,)),
        ],
        compiler_params=pltpu.CompilerParams(vmem_limit_bytes=50 * MIB),
        cost_estimate=pl.CostEstimate(flops=8 * 10**9, bytes_accessed=8 * MIB, transcendentals=5 * 10**6),
    )(col_arr, recv, *ups, q_bias, k_bias, v_bias, cos_table, sin_table)


def per_device(q_load, k_load, v_load, q_bias, k_bias, v_bias, place, segment, d_context):
    col = lax.axis_index("col")
    row = lax.axis_index("row")
    j = col % 4
    col_arr = col.reshape(1).astype(jnp.int32)
    smem = pl.BlockSpec(memory_space=pltpu.SMEM)

    packed = pl.pallas_call(
        pack_kernel,
        out_shape=shape((8, KV_HEADS, 16, SENT), BF16),
        in_specs=[any_spec()] * 5,
        out_specs=any_spec(),
        scratch_shapes=[
            pltpu.VMEM((TOK, Q_WIDTH), BF16),
            pltpu.VMEM((TOK, KV_WIDTH), BF16),
            pltpu.VMEM((TOK, KV_WIDTH), BF16),
            pltpu.VMEM((1, TOK), jnp.int32),
            pltpu.VMEM((1, TOK), jnp.int32),
            pltpu.VMEM((8, KV_HEADS, 16, SENT), BF16),
            pltpu.SemaphoreType.DMA((12,)),
        ],
        compiler_params=pltpu.CompilerParams(vmem_limit_bytes=60 * MIB),
        cost_estimate=pl.CostEstimate(flops=2 * 128 * 128 * 5120, bytes_accessed=5 * MIB, transcendentals=0),
    )(q_load[0], k_load[0], v_load[0], place, segment)
    recv = lax.all_to_all(
        packed.reshape(32, 16, SENT), "col", split_axis=0, concat_axis=0, tiled=True
    )

    up_own = d_context[0]
    ups = []
    for s in range(4):
        piece = lax.dynamic_slice_in_dim(up_own, PART * (j ^ s), PART, 1)
        ups.append(piece if s == 0 else swap(piece, "col", s, 32))
    attended = attend(
        col_arr, recv.reshape(SLAB, SENT), ups,
        q_bias.reshape(1, Q_WIDTH), k_bias.reshape(1, KV_WIDTH), v_bias.reshape(1, KV_WIDTH),
    )
    ctx_parts, back, bias = attended[:4], attended[4], attended[5]
    returned = lax.all_to_all(
        back.reshape(32, 16, BACK), "col", split_axis=0, concat_axis=0, tiled=True
    )
    ctx_in = [ctx_parts[0], swap(ctx_parts[1], "col", 1, 32)]
    ctx_in += [swap(ctx_parts[2], "col", 2, 32), swap(ctx_parts[3], "col", 3, 32)]
    for step in (2, 4):
        bias = bias + swap(bias, "row", step, 8)
    bias, ctx_in[2], ctx_in[3] = lax.optimization_barrier((bias, ctx_in[2], ctx_in[3]))
    context = pl.pallas_call(
        join_kernel,
        out_shape=shape((TOK, Q_WIDTH), BF16),
        in_specs=[smem] + [vmem_spec()] * 4,
        out_specs=vmem_spec(),
        compiler_params=pltpu.CompilerParams(vmem_limit_bytes=16 * MIB),
        cost_estimate=pl.CostEstimate(flops=0, bytes_accessed=2 * MIB, transcendentals=0),
    )(col_arr, *ctx_in)
    bias = bias + swap(bias, "row", 1, 8)
    bias, context = lax.optimization_barrier((bias, context))
    bias = jnp.where(j == row // 2, bias, 0.0)
    for step in (1, 2):
        bias = bias + swap(bias, "col", step, 32)
    bias = bias + (swap(bias, "col", 8, 32) + swap(bias, "col", 16, 32) + swap(bias, "col", 24, 32))
    other = swap(bias, "col", 4, 32)
    grad_q, grad_k, grad_v = pl.pallas_call(
        unpack_kernel,
        out_shape=[shape((TOK, Q_WIDTH), BF16), shape((TOK, KV_WIDTH), BF16), shape((TOK, KV_WIDTH), BF16)],
        in_specs=[vmem_spec()] * 2,
        out_specs=[vmem_spec()] * 3,
        scratch_shapes=[
            pltpu.VMEM((TOK, PART), BF16),
            pltpu.VMEM((TOK, KV_WIDTH), BF16),
            pltpu.VMEM((TOK, KV_WIDTH), BF16),
        ],
        compiler_params=pltpu.CompilerParams(vmem_limit_bytes=24 * MIB),
        cost_estimate=pl.CostEstimate(flops=2 * 128 * 128 * 5120, bytes_accessed=4 * MIB, transcendentals=0),
    )(returned, place)
    other, grad_v = lax.optimization_barrier((other, grad_v))
    bias_q, bias_kv = pl.pallas_call(
        finish_kernel,
        out_shape=[shape((1, 16), F32), shape((2, 2), F32)],
        in_specs=[smem, vmem_spec(), vmem_spec()],
        out_specs=[vmem_spec()] * 2,
        compiler_params=pltpu.CompilerParams(vmem_limit_bytes=8 * MIB),
        cost_estimate=pl.CostEstimate(flops=0, bytes_accessed=32768, transcendentals=0),
    )(jnp.stack([col, row]).astype(jnp.int32), bias, other)
    bias_q = bias_q.reshape(16)
    return (context[None], grad_q[None], grad_k[None], grad_v[None], bias_q, bias_kv)


def solution(mesh):
    return jax.shard_map(
        per_device,
        mesh=mesh,
        in_specs=(
            P("row", "col", None),
            P("row", "col", None),
            P("row", "col", None),
            P(),
            P(),
            P(),
            P("row", "col"),
            P("row", "col"),
            P("row", "col", None),
        ),
        out_specs=(
            P("row", "col", None),
            P("row", "col", None),
            P("row", "col", None),
            P("row", "col", None),
            P(("row", "col")),
            P(None, ("row", "col")),
        ),
        check_vma=False,
    )
```
